256 devices in a mesh: batch: 16 (over z, x_hi), row: 4 (over y), col: 4 (over x_lo, core).
Axes of the slice: x: 4 (x_hi: 2, x_lo: 2; x = x_hi * 2 + x_lo), y: 4, z: 8, core: 2. Of those that a mesh axis runs over, the one named last changes fastest.
Arguments:
- latent: bfloat16 [1024, 64, 640], P(('batch', 'row'), 'col'), parts along dimension 0, may hold values from -40 to 40
- norm1_gain: float32 [640], replicated, may hold values from 0.1 to 1.9
- norm1_shift: float32 [640], replicated, may hold values from -3 to 3
- conv_weight: bfloat16 [3, 3, 640, 640], replicated, may hold values from -0.078125 to 0.078125
- norm2_gain: float32 [640], replicated, may hold values from 0.1 to 1.9
- norm2_shift: float32 [640], replicated, may hold values from -3 to 3
- w_query: bfloat16 [640, 640], replicated, may hold values from -1 to 1
- w_key: bfloat16 [640, 640], replicated, may hold values from -1 to 1
- w_value: bfloat16 [640, 640], replicated, may hold values from -0.25 to 0.25
- w_out: bfloat16 [640, 640], replicated, may hold values from -0.25 to 0.25
Outputs:
- conv_update: bfloat16 [1024, 64, 640], P(('batch', 'row'), 'col'), parts along dimension 0
- attn_update: bfloat16 [1024, 64, 640], P(('batch', 'row'), 'col'), parts along dimension 0
The draws below stay inside these ranges and needn't reach their ends.
There are 16 independent parts, one for each index of `batch`. The reference program is written for one: setup_inputs(seed, part) draws one part's arguments, and reference() takes and returns one part's arrays. A program takes and returns all parts, laid end to end along the dimension named above; an argument that names none is the same for every part. Nothing has to cross between parts.
All inputs are finite; a program needn't handle non-finite values.
Results may differ from the reference program's by a relative error of at most 0.04.
Values may be sent and summed in bfloat16 or wider, within the bound.
No kernel may reach another device: no remote copies, remote signals or barrier semaphores. Data moves between devices by JAX's collectives and lax.ppermute only.
A program may use at most 64 MiB of HBM per device.

```python
import math
import jax
import jax.numpy as jnp
from jax import lax

C = 640
GROUPS = 32
HEAD = 64
NH = 64
NW = 64


def shared_query(key):
    return jnp.clip(jax.random.normal(key, (C, C), jnp.float32), -4.0, 4.0)


def draw_w_query(key, part):
    common = shared_query(key)
    return (common * math.sqrt(3.0 / C)).astype(jnp.bfloat16)


def draw_w_key(key, part):
    key = jax.random.fold_in(key, 8)
    own_draw = jnp.clip(jax.random.normal(key, (C, C), jnp.float32), -4.0, 4.0)
    mixed = own_draw
    return (mixed * math.sqrt(3.0 / C)).astype(jnp.bfloat16)


def spatial_ramp(factor):
    row_pos = jnp.arange(NH, dtype=jnp.float32) / max(NH - 1, 1)
    col_pos = jnp.arange(NW, dtype=jnp.float32) / max(NW - 1, 1)
    return (factor ** (row_pos - 0.5))[:, None] * (factor ** (col_pos - 0.5))[None, :]


def draw_latent(key, part):
    key = jax.random.fold_in(key, 1)
    key_base, key_scale, key_mean = jax.random.split(key, 3)
    channel_scale = jnp.exp(jax.random.uniform(key_scale, (C,), jnp.float32, math.log(0.3), math.log(2.5)))
    spatial = spatial_ramp(3.0)
    offset = jnp.clip(0.8 * jax.random.normal(key_mean, (C,), jnp.float32), -1.2, 1.2)
    base = jnp.clip(jax.random.normal(key_base, (NH, NW, C), jnp.float32), -4.0, 4.0) + offset
    grid = base * channel_scale * spatial[:, :, None]
    return grid.astype(jnp.bfloat16)


def centred(key, shape, scale, limit, held_as=jnp.bfloat16):
    return jnp.clip(scale * jax.random.normal(key, shape, jnp.float32), -limit, limit).astype(held_as)


def setup_inputs(seed: int = 0, part: int = 0) -> dict:
    splits = jax.random.split(jax.random.key(seed), 11)
    own_keys = jax.random.split(jax.random.fold_in(splits[10], part), 11)
    return {
        "latent": draw_latent(jax.random.fold_in(jax.random.fold_in(splits[10], part), 71), part),
        "norm1_gain": jnp.clip(1.0 + 0.18 * jax.random.normal(splits[1], (C,), jnp.float32), 0.1, 1.9),
        "norm1_shift": centred(splits[2], (C,), 0.5, 3.0, jnp.float32),
        "conv_weight": centred(splits[3], (3, 3, C, C), (9 * C) ** -0.5, 0.078125),
        "norm2_gain": jnp.clip(1.0 + 0.18 * jax.random.normal(splits[4], (C,), jnp.float32), 0.1, 1.9),
        "norm2_shift": centred(splits[5], (C,), 0.5, 3.0, jnp.float32),
        "w_query": draw_w_query(jax.random.fold_in(splits[10], 71), part),
        "w_key": draw_w_key(jax.random.fold_in(splits[10], 71), part),
        "w_value": centred(splits[8], (C, C), C ** -0.5, 0.25),
        "w_out": centred(splits[9], (C, C), C ** -0.5, 0.25),
    }


def group_norm(values, scale_vec, shift_vec):
    flat = values.astype(jnp.float32).reshape(NH * NW, GROUPS, C // GROUPS)
    means = lax.optimization_barrier(jnp.mean(flat, axis=(0, 2), keepdims=True))
    deviation = flat - means
    spread = lax.optimization_barrier(jnp.mean(deviation * deviation, axis=(0, 2), keepdims=True))
    normal_form = deviation / jnp.sqrt(spread + 1e-05)
    return normal_form.reshape(NH, NW, C) * scale_vec + shift_vec

def one_head(triple):
    q_rows, k_rows, v_rows = triple
    scores = jnp.dot(q_rows, k_rows.T, preferred_element_type=jnp.float32) * 0.125
    row_top = lax.optimization_barrier(jnp.max(scores, axis=1, keepdims=True))
    exponent = jnp.exp(scores - row_top)
    weights = exponent.astype(jnp.bfloat16)
    summed = jnp.dot(weights, v_rows, preferred_element_type=jnp.float32)
    return summed / lax.optimization_barrier(jnp.sum(exponent, axis=1, keepdims=True))

def reference(latent, norm1_gain, norm1_shift, conv_weight, norm2_gain, norm2_shift, w_query, w_key, w_value, w_out):
    act = jax.nn.silu(group_norm(latent, norm1_gain, norm1_shift)).astype(jnp.bfloat16)
    padded = jnp.pad(act, ((1, 1), (1, 1), (0, 0)))
    summed = jnp.zeros((NH * NW, C), jnp.float32)
    for tap_row in range(3):
        for tap_col in range(3):
            window = padded[tap_row:tap_row + NH, tap_col:tap_col + NW].reshape(NH * NW, C)
            summed = summed + jnp.dot(window, conv_weight[tap_row, tap_col], preferred_element_type=jnp.float32)
    conv_update = summed.reshape(NH, NW, C).astype(jnp.bfloat16)
    stream = (latent.astype(jnp.float32) + conv_update.astype(jnp.float32)).astype(jnp.bfloat16)
    normed = group_norm(stream, norm2_gain, norm2_shift).astype(jnp.bfloat16).reshape(NH * NW, C)
    queries = jnp.dot(normed, w_query, preferred_element_type=jnp.float32).astype(jnp.bfloat16)
    key_rows = jnp.dot(normed, w_key, preferred_element_type=jnp.float32).astype(jnp.bfloat16)
    value_rows = jnp.dot(normed, w_value, preferred_element_type=jnp.float32).astype(jnp.bfloat16)
    head_count = C // HEAD

    def split_heads(matrix):
        return matrix.reshape(NH * NW, head_count, HEAD).transpose(1, 0, 2)
    outputs = lax.map(one_head, (split_heads(queries), split_heads(key_rows), split_heads(value_rows)))
    attended = outputs.transpose(1, 0, 2).reshape(NH * NW, C).astype(jnp.bfloat16)
    attn_update = jnp.dot(attended, w_out, preferred_element_type=jnp.float32).astype(jnp.bfloat16)
    return (conv_update, attn_update.reshape(NH, NW, C))
```

```python
import math

import jax
import jax.numpy as jnp
from jax import lax
from jax.experimental import pallas as pl
from jax.experimental.pallas import tpu as pltpu
from jax.sharding import Mesh
from jax.sharding import PartitionSpec as P

GROUPS = 32
HEAD = 64
EPS = 1e-05
F32 = jnp.float32
BF16 = jnp.bfloat16
NT = (((1,), (1,)), ((), ()))
TN = (((0,), (0,)), ((), ()))
PARTS = ("row", "x", "core")
VMEM_LIMIT = 48 * 2**20
HEADROOM = 64.0


def params(limit=VMEM_LIMIT):
    return pltpu.CompilerParams(vmem_limit_bytes=limit)


def local_moments(values):
    count = values.shape[0]
    mean = jnp.sum(values, axis=0, keepdims=True) * (1.0 / count)
    deviation = values - mean
    return jnp.concatenate([mean, jnp.sum(deviation * deviation, axis=0, keepdims=True)], axis=0)


def combine_moments(gathered, local_count):
    devices, _, channels = gathered.shape
    per_group = channels // GROUPS
    means = gathered[:, 0, :]
    mean_c = jnp.sum(means, axis=0, keepdims=True) * (1.0 / devices)
    off = means - mean_c
    square_c = jnp.sum(gathered[:, 1, :], axis=0, keepdims=True) + local_count * jnp.sum(
        off * off, axis=0, keepdims=True
    )
    row_of = lax.broadcasted_iota(jnp.int32, (channels, channels), 0).astype(F32)
    col_of = lax.broadcasted_iota(jnp.int32, (channels, channels), 1).astype(F32)
    group_row = jnp.floor((row_of + 0.5) * (1.0 / per_group))
    group_col = jnp.floor((col_of + 0.5) * (1.0 / per_group))
    same = jnp.where(group_row == group_col, 1.0, 0.0).astype(F32)

    def group_sum(vec):
        wide = jnp.broadcast_to(vec, (8, channels))
        return jnp.dot(
            wide, same, precision=lax.Precision.HIGHEST, preferred_element_type=F32
        )[0:1]

    mean_g = group_sum(mean_c) * (1.0 / per_group)
    gap = mean_c - mean_g
    pixels = devices * local_count
    square_g = group_sum(square_c + pixels * (gap * gap))
    spread = square_g * (1.0 / (pixels * per_group))
    return mean_g, 1.0 / jnp.sqrt(spread + EPS)


def moments_kernel(lat_ref, out_ref):
    values = lat_ref[...].reshape(-1, lat_ref.shape[-1]).astype(F32)
    out_ref[...] = jnp.broadcast_to(local_moments(values)[None], out_ref.shape)


def conv_kernel(
    edge_ref, lat_ref, top_ref, bot_ref, left_ref, right_ref, stat_ref, gain_ref, shift_ref, w_hbm,
    conv_ref, stream_ref, out_stat_ref, w_ref, sems,
):
    rows, cols, channels = lat_ref.shape
    depth = 3 * channels
    copies = [
        pltpu.make_async_copy(
            w_hbm.at[pl.ds(t * depth, depth)], w_ref.at[pl.ds(t * depth, depth)], sems.at[t]
        )
        for t in range(3)
    ]
    for copy in copies:
        copy.start()
    mean, inv = combine_moments(stat_ref[...], rows * cols)
    scale = inv * gain_ref[...]
    shift = shift_ref[...]

    def act(raw):
        u = (raw.astype(F32) - mean[None]) * scale[None] + shift[None]
        return u / (1.0 + jnp.exp(-u))

    keep = [jnp.where(edge_ref[i] > 0, 1.0, 0.0).astype(F32) for i in range(4)]
    middle = act(lat_ref[...])
    above = act(top_ref[...]) * keep[0]
    below = act(bot_ref[...]) * keep[1]
    tall = jnp.concatenate([above, middle, below], axis=0)

    def side(ref, flag):
        v = act(ref[...]) * flag
        return jnp.concatenate([v[:1] * keep[0], v[1 : rows + 1], v[rows + 1 :] * keep[1]], axis=0)

    left = side(left_ref, keep[2])
    right = side(right_ref, keep[3])
    shifted = [
        jnp.concatenate([left, tall[:, : cols - 1]], axis=1).astype(BF16),
        tall.astype(BF16),
        jnp.concatenate([tall[:, 1:], right], axis=1).astype(BF16),
    ]
    total = None
    for t in range(3):
        window = jnp.concatenate(
            [s[t : t + rows].reshape(rows * cols, channels) for s in shifted], axis=1
        )
        copies[t].wait()
        part = jnp.dot(window, w_ref[pl.ds(t * depth, depth), :], preferred_element_type=F32)
        total = part if total is None else total + part
    update = total.astype(BF16)
    conv_ref[...] = update.reshape(rows, cols, channels)
    stream = (
        lat_ref[...].reshape(rows * cols, channels).astype(F32) + update.astype(F32)
    ).astype(BF16)
    stream_ref[...] = stream
    out_stat_ref[...] = jnp.broadcast_to(
        local_moments(stream.astype(F32))[None], out_stat_ref.shape
    )


def normalise(block, affine):
    return ((block.astype(F32) - affine[0:1]) * affine[1:2] + affine[2:3]).astype(BF16)


def project(blocks, affine, wk_ref, wvt_ref):
    raw = jnp.concatenate(blocks, axis=0) if len(blocks) > 1 else blocks[0]
    normed = normalise(raw, affine)
    keys = jnp.dot(normed, wk_ref[...], preferred_element_type=F32).astype(BF16)
    values = lax.dot_general(wvt_ref[...], normed, NT, preferred_element_type=F32).astype(BF16)
    return keys, values


def weighted(values, weights, pair, acc_of):
    length = values.shape[1]
    queries = weights.shape[1] // 2
    ones = jnp.ones((16, length), BF16)
    for h in range(2):
        low = 2 * HEAD * pair + HEAD * h
        stack = jnp.concatenate([values[low : low + HEAD], ones], axis=0)
        acc_of(2 * pair + h, jnp.dot(
            stack, weights[:, h * queries : (h + 1) * queries], preferred_element_type=F32
        ))


def first_kernel(
    own_ref, peer_ref, stat_ref, gain_ref, shift_ref, wqt_ref, wk_ref, wvt_ref,
    aff_ref, qbd_ref, acc_ref, max_ref,
):
    queries, channels = own_ref.shape
    pairs = channels // (2 * HEAD)
    mean, inv = combine_moments(stat_ref[...], queries)
    affine = jnp.concatenate(
        [mean, inv * gain_ref[...], shift_ref[...], jnp.zeros((5, channels), F32)], axis=0
    )
    aff_ref[...] = affine
    own = own_ref[...]
    normed = normalise(own, affine)
    factor = math.log2(math.e) / math.sqrt(HEAD)
    qt = (
        lax.dot_general(wqt_ref[...], normed, NT, preferred_element_type=F32) * factor
    ).astype(BF16)
    zero = jnp.zeros((HEAD, queries), BF16)
    keys, values = project([own, peer_ref[...]], affine, wk_ref, wvt_ref)
    for j in range(pairs):
        low = 2 * HEAD * j
        qbd = jnp.concatenate(
            [
                jnp.concatenate([qt[low : low + HEAD], zero], axis=1),
                jnp.concatenate([zero, qt[low + HEAD : low + 2 * HEAD]], axis=1),
            ],
            axis=0,
        )
        qbd_ref[j] = qbd
        scores = jnp.dot(keys[:, low : low + 2 * HEAD], qbd, preferred_element_type=F32)
        top = jnp.max(scores, axis=0, keepdims=True)
        max_ref[j] = top
        weights = jnp.exp2(scores - top).astype(BF16)

        def put(head, value):
            acc_ref[head] = value

        weighted(values, weights, j, put)


def more_kernel(count, last, *refs):
    blocks = refs[:count]
    aff_ref, qbd_ref, acc_in, max_in, wk_ref, wvt_ref = refs[count : count + 6]
    rest = refs[count + 6 :]
    if last:
        wo_ref, out_ref, acc_ref = rest
        max_ref = None
    else:
        acc_ref, max_ref = rest
    heads, _, queries = acc_in.shape
    pairs = heads // 2
    affine = aff_ref[...]
    run = [None] * pairs
    for g in range(0, count, 2):
        keys, values = project([blocks[g][...], blocks[g + 1][...]], affine, wk_ref, wvt_ref)
        for j in range(pairs):
            low = 2 * HEAD * j
            scores = jnp.dot(keys[:, low : low + 2 * HEAD], qbd_ref[j], preferred_element_type=F32)
            top = jnp.max(scores.reshape(-1, 8, 2 * queries), axis=0)
            run[j] = top if run[j] is None else jnp.maximum(run[j], top)
            weights = jnp.exp2(scores - max_in[j]).astype(BF16)

            def put(head, value, first=(g == 0)):
                acc_ref[head] = (acc_in[head] if first else acc_ref[head]) + value

            weighted(values, weights, j, put)
    excess = run[0] - max_in[0]
    for j in range(1, pairs):
        excess = jnp.maximum(excess, run[j] - max_in[j])
    over = jnp.max(excess) > HEADROOM
    if not last:
        max_ref[...] = max_in[...]

    @pl.when(over)
    def _():
        acc_ref[...] = acc_in[...]
        for j in range(pairs):
            low = 2 * HEAD * j
            top = max_in[j]
            for g in range(count):
                keys, values = project([blocks[g][...]], affine, wk_ref, wvt_ref)
                scores = jnp.dot(
                    keys[:, low : low + 2 * HEAD], qbd_ref[j], preferred_element_type=F32
                )
                new = jnp.maximum(top, jnp.max(scores, axis=0, keepdims=True))
                rescale = jnp.exp2(top - new)
                weights = jnp.exp2(scores - new).astype(BF16)

                def put(head, value, j=j, rescale=rescale):
                    h = head - 2 * j
                    acc_ref[head] = (
                        acc_ref[head] * rescale[:, h * queries : (h + 1) * queries] + value
                    )

                weighted(values, weights, j, put)
                top = new
            if not last:
                max_ref[j] = top

    if last:
        parts = []
        for h in range(heads):
            acc = acc_ref[h]
            parts.append((acc[:HEAD] / acc[HEAD : HEAD + 1]).astype(BF16))
        attended = jnp.concatenate(parts, axis=0)
        out_ref[...] = lax.dot_general(
            attended, wo_ref[...], TN, preferred_element_type=F32
        ).astype(BF16)


def shift_by(value, axis, step):
    count = lax.axis_size(axis)
    return lax.ppermute(value, axis, [(i, (i + step) % count) for i in range(count)])


def shards(
    latent, norm1_gain, norm1_shift, conv_weight, norm2_gain, norm2_shift,
    w_query, w_key, w_value, w_out,
):
    rows, cols, channels = latent.shape
    local = rows * cols
    heads = channels // HEAD
    pairs = heads // 2
    devices = math.prod(lax.axis_size(a) for a in PARTS)
    sds = jax.ShapeDtypeStruct
    vec = lambda v: v.reshape(1, channels)

    moments = pl.pallas_call(
        moments_kernel, out_shape=sds((devices, 2, channels), F32), compiler_params=params()
    )(latent)
    gathered = lax.all_to_all(moments, PARTS, 0, 0)

    def neighbours(low_edge, high_edge, axis):
        count = math.prod(lax.axis_size(a) for a in axis)
        forward = [(i, i + 1) for i in range(count - 1)]
        backward = [(b, a) for a, b in forward]
        return lax.ppermute(high_edge, axis, forward), lax.ppermute(low_edge, axis, backward)

    top, bot = neighbours(latent[:1], latent[-1:], ("row",))
    tall = lambda i: jnp.concatenate([top[:, i : i + 1], latent[:, i : i + 1], bot[:, i : i + 1]], 0)
    left, right = neighbours(tall(0), tall(cols - 1), ("x", "core"))
    row = lax.axis_index("row")
    col = lax.axis_index(("x", "core"))
    edges = jnp.stack(
        [row > 0, row < lax.axis_size("row") - 1, col > 0,
         col < lax.axis_size("x") * lax.axis_size("core") - 1]
    ).astype(jnp.int32)
    vm = pl.BlockSpec(memory_space=pltpu.VMEM)
    conv_update, stream, moments2 = pl.pallas_call(
        conv_kernel,
        in_specs=[pl.BlockSpec(memory_space=pltpu.SMEM)] + [vm] * 8
        + [pl.BlockSpec(memory_space=pl.ANY)],
        out_specs=[vm] * 3,
        out_shape=[
            sds((rows, cols, channels), BF16),
            sds((local, channels), BF16),
            sds((devices, 2, channels), F32),
        ],
        scratch_shapes=[
            pltpu.VMEM((9 * channels, channels), BF16), pltpu.SemaphoreType.DMA((3,))
        ],
        compiler_params=params(),
    )(
        edges, latent, top, bot, left, right, gathered, vec(norm1_gain), vec(norm1_shift),
        conv_weight.reshape(9 * channels, channels),
    )

    swap = lambda v: shift_by(v, "core", 1)
    cross = lambda v: shift_by(v, "x", 1)
    up = lambda v: shift_by(v, "row", 1)
    down = lambda v: shift_by(v, "row", -1)
    own_peer = swap(stream)
    x0, ym, yp = cross(stream), up(stream), down(stream)
    gathered2 = lax.all_to_all(moments2, PARTS, 0, 0)
    x0_peer, ym_peer, yp_peer = swap(x0), swap(ym), swap(yp)
    xm, y2, xp = cross(ym), up(ym), down(x0)
    xm_peer, y2_peer, xp_peer = swap(xm), swap(y2), swap(xp)
    x2 = cross(y2)
    x2_peer = swap(x2)

    wqt, wvt = w_query.T, w_value.T
    state = [
        sds((8, channels), F32),
        sds((pairs, 2 * HEAD, 2 * local), BF16),
        sds((heads, HEAD + 16, local), F32),
        sds((pairs, 1, 2 * local), F32),
    ]
    affine, qbd, acc, top_scores = pl.pallas_call(
        first_kernel, out_shape=state, compiler_params=params()
    )(stream, own_peer, gathered2, vec(norm2_gain), vec(norm2_shift), wqt, w_key, wvt)

    def more(blocks, acc, top_scores, last):
        kernel = lambda *refs: more_kernel(len(blocks), last, *refs)
        args = [*blocks, affine, qbd, acc, top_scores, w_key, wvt]
        if not last:
            return pl.pallas_call(kernel, out_shape=state[2:], compiler_params=params())(*args)
        return pl.pallas_call(
            kernel,
            out_shape=sds((local, channels), BF16),
            scratch_shapes=[pltpu.VMEM((heads, HEAD + 16, local), F32)],
            compiler_params=params(),
        )(*args, w_out)

    acc, top_scores = more([x0, x0_peer, ym, ym_peer, yp, yp_peer], acc, top_scores, False)
    attn = more(
        [xm, xm_peer, y2, y2_peer, xp, xp_peer, x2, x2_peer], acc, top_scores, True
    )
    return conv_update, attn.reshape(rows, cols, channels)


def solution(mesh):
    sizes = dict(mesh.shape)
    split = Mesh(
        mesh.devices.reshape(sizes["batch"], sizes["row"], sizes["col"] // 2, 2),
        ("batch", "row", "x", "core"),
    )
    tiles = P(("batch", "row"), ("x", "core"), None)
    return jax.shard_map(
        shards,
        mesh=split,
        in_specs=(tiles,) + (P(),) * 9,
        out_specs=(tiles, tiles),
        check_vma=False,
    )
```

```python
import math

import jax
import jax.numpy as jnp
from jax import lax
from jax.experimental import pallas as pl
from jax.experimental.pallas import tpu as pltpu
from jax.sharding import Mesh
from jax.sharding import PartitionSpec as P

GROUPS = 32
HEAD = 64
EPS = 1e-05
F32 = jnp.float32
BF16 = jnp.bfloat16
NT = (((1,), (1,)), ((), ()))
TN = (((0,), (0,)), ((), ()))
PARTS = ("row", "x", "core")
VMEM_LIMIT = 28 * 2**20
HEADROOM = 64.0


def params(limit=VMEM_LIMIT):
    return pltpu.CompilerParams(vmem_limit_bytes=limit)


def local_moments(values):
    count = values.shape[0]
    mean = jnp.sum(values, axis=0, keepdims=True) * (1.0 / count)
    deviation = values - mean
    return jnp.concatenate([mean, jnp.sum(deviation * deviation, axis=0, keepdims=True)], axis=0)


def combine_moments(gathered, local_count):
    devices, _, channels = gathered.shape
    per_group = channels // GROUPS
    means = gathered[:, 0, :]
    mean_c = jnp.sum(means, axis=0, keepdims=True) * (1.0 / devices)
    off = means - mean_c
    square_c = jnp.sum(gathered[:, 1, :], axis=0, keepdims=True) + local_count * jnp.sum(
        off * off, axis=0, keepdims=True
    )
    row_of = lax.broadcasted_iota(jnp.int32, (channels, channels), 0).astype(F32)
    col_of = lax.broadcasted_iota(jnp.int32, (channels, channels), 1).astype(F32)
    group_row = jnp.floor((row_of + 0.5) * (1.0 / per_group))
    group_col = jnp.floor((col_of + 0.5) * (1.0 / per_group))
    same = jnp.where(group_row == group_col, 1.0, 0.0).astype(F32)

    def group_sum(vec):
        wide = jnp.broadcast_to(vec, (8, channels))
        return jnp.dot(
            wide, same, precision=lax.Precision.HIGHEST, preferred_element_type=F32
        )[0:1]

    mean_g = group_sum(mean_c) * (1.0 / per_group)
    gap = mean_c - mean_g
    pixels = devices * local_count
    square_g = group_sum(square_c + pixels * (gap * gap))
    spread = square_g * (1.0 / (pixels * per_group))
    return mean_g, 1.0 / jnp.sqrt(spread + EPS)


def moments_kernel(lat_ref, out_ref):
    values = lat_ref[...].reshape(-1, lat_ref.shape[-1]).astype(F32)
    out_ref[...] = jnp.broadcast_to(local_moments(values)[None], out_ref.shape)


def conv_kernel(
    edge_ref, lat_ref, top_ref, bot_ref, left_ref, right_ref, stat_ref, gain_ref, shift_ref, w_hbm,
    conv_ref, stream_ref, out_stat_ref, w_ref, sems,
):
    rows, cols, channels = lat_ref.shape
    depth = 3 * channels
    copies = [
        pltpu.make_async_copy(
            w_hbm.at[pl.ds(t * depth, depth)], w_ref.at[pl.ds(t * depth, depth)], sems.at[t]
        )
        for t in range(3)
    ]
    for copy in copies:
        copy.start()
    mean, inv = combine_moments(stat_ref[...], rows * cols)
    scale = inv * gain_ref[...]
    shift = shift_ref[...]

    def act(raw):
        u = (raw.astype(F32) - mean[None]) * scale[None] + shift[None]
        return u / (1.0 + jnp.exp(-u))

    keep = [jnp.where(edge_ref[i] > 0, 1.0, 0.0).astype(F32) for i in range(4)]
    middle = act(lat_ref[...])
    above = act(top_ref[...]) * keep[0]
    below = act(bot_ref[...]) * keep[1]
    tall = jnp.concatenate([above, middle, below], axis=0)

    def side(ref, flag):
        v = act(ref[...]) * flag
        return jnp.concatenate([v[:1] * keep[0], v[1 : rows + 1], v[rows + 1 :] * keep[1]], axis=0)

    left = side(left_ref, keep[2])
    right = side(right_ref, keep[3])
    shifted = [
        jnp.concatenate([left, tall[:, : cols - 1]], axis=1).astype(BF16),
        tall.astype(BF16),
        jnp.concatenate([tall[:, 1:], right], axis=1).astype(BF16),
    ]
    total = None
    for t in range(3):
        window = jnp.concatenate(
            [s[t : t + rows].reshape(rows * cols, channels) for s in shifted], axis=1
        )
        copies[t].wait()
        part = jnp.dot(window, w_ref[pl.ds(t * depth, depth), :], preferred_element_type=F32)
        total = part if total is None else total + part
    update = total.astype(BF16)
    conv_ref[...] = update.reshape(rows, cols, channels)
    stream = (
        lat_ref[...].reshape(rows * cols, channels).astype(F32) + update.astype(F32)
    ).astype(BF16)
    stream_ref[...] = stream
    out_stat_ref[...] = jnp.broadcast_to(
        local_moments(stream.astype(F32))[None], out_stat_ref.shape
    )


def normalise(block, affine):
    return ((block.astype(F32) - affine[0:1]) * affine[1:2] + affine[2:3]).astype(BF16)


def project(blocks, affine, wk_ref, wvt_ref, key_ref, value_ref):
    raw = jnp.concatenate(blocks, axis=0) if len(blocks) > 1 else blocks[0]
    normed = normalise(raw, affine)
    key_ref[...] = jnp.dot(normed, wk_ref[...], preferred_element_type=F32).astype(BF16)
    value_ref[...] = lax.dot_general(
        wvt_ref[...], normed, NT, preferred_element_type=F32
    ).astype(BF16)


def stacked(values):
    return jnp.concatenate([values, jnp.ones((16, values.shape[1]), BF16)], axis=0)


def first_kernel(
    own_ref, peer_ref, stat_ref, gain_ref, shift_ref, wqt_ref, wk_ref, wvt_ref,
    aff_ref, qbd_ref, acc_ref, max_ref, key_ref, value_ref,
):
    length, channels = own_ref.shape
    pairs = channels // (2 * HEAD)
    queries = 2 * length
    mean, inv = combine_moments(stat_ref[...], length)
    affine = jnp.concatenate(
        [mean, inv * gain_ref[...], shift_ref[...], jnp.zeros((5, channels), F32)], axis=0
    )
    aff_ref[...] = affine
    own = own_ref[...]
    normed = normalise(jnp.concatenate([own, peer_ref[...]], axis=0), affine)
    factor = math.log2(math.e) / math.sqrt(HEAD)
    qt = (
        lax.dot_general(wqt_ref[...], normed, NT, preferred_element_type=F32) * factor
    ).astype(BF16)
    zero = jnp.zeros((HEAD, queries), BF16)
    project([own], affine, wk_ref, wvt_ref, key_ref, value_ref)
    for j in range(pairs):
        low = 2 * HEAD * j
        qbd = jnp.concatenate(
            [
                jnp.concatenate([qt[low : low + HEAD], zero], axis=1),
                jnp.concatenate([zero, qt[low + HEAD : low + 2 * HEAD]], axis=1),
            ],
            axis=0,
        )
        qbd_ref[j] = qbd
        scores = jnp.dot(key_ref[:, low : low + 2 * HEAD], qbd, preferred_element_type=F32)
        top = jnp.max(scores, axis=0, keepdims=True)
        max_ref[j] = top
        weights = jnp.exp2(scores - top).astype(BF16)
        for h in range(2):
            acc_ref[2 * j + h] = jnp.dot(
                stacked(value_ref[low + HEAD * h : low + HEAD * h + HEAD]),
                weights[:, h * queries : (h + 1) * queries],
                preferred_element_type=F32,
            )


def more_kernel(count, last, *refs):
    blocks = refs[:count]
    aff_ref, qbd_ref, acc_in, max_in, wk_ref, wvt_ref, acc_ref, max_ref = refs[count : count + 8]
    if last:
        give_ref, key_ref, value_ref = refs[count + 8 :]
    else:
        key_ref, value_ref = refs[count + 8 :]
    heads, _, queries = acc_in.shape
    pairs = heads // 2
    project([b[...] for b in blocks], aff_ref[...], wk_ref, wvt_ref, key_ref, value_ref)
    excess = None
    for j in range(pairs):
        low = 2 * HEAD * j
        scores = jnp.dot(
            key_ref[:, low : low + 2 * HEAD], qbd_ref[j], preferred_element_type=F32
        )
        over = jnp.max(scores.reshape(-1, 8, 2 * queries), axis=0) - max_in[j]
        excess = over if excess is None else jnp.maximum(excess, over)
        weights = jnp.exp2(scores - max_in[j]).astype(BF16)
        for h in range(2):
            acc_ref[2 * j + h] = acc_in[2 * j + h] + jnp.dot(
                stacked(value_ref[low + HEAD * h : low + HEAD * h + HEAD]),
                weights[:, h * queries : (h + 1) * queries],
                preferred_element_type=F32,
            )
    max_ref[...] = max_in[...]

    @pl.when(jnp.max(excess) > HEADROOM)
    def _():
        def one_pair(j, _):
            low = pl.multiple_of(2 * HEAD * j, 2 * HEAD)
            scores = jnp.dot(
                key_ref[:, pl.ds(low, 2 * HEAD)], qbd_ref[j], preferred_element_type=F32
            )
            top = max_in[j]
            new = jnp.maximum(top, jnp.max(scores, axis=0, keepdims=True))
            rescale = jnp.exp2(top - new)
            weights = jnp.exp2(scores - new).astype(BF16)
            for h in range(2):
                acc_ref[2 * j + h] = acc_in[2 * j + h] * rescale[
                    :, h * queries : (h + 1) * queries
                ] + jnp.dot(
                    stacked(value_ref[pl.ds(low + HEAD * h, HEAD)]),
                    weights[:, h * queries : (h + 1) * queries],
                    preferred_element_type=F32,
                )
            max_ref[j] = new
            return 0

        lax.fori_loop(0, pairs, one_pair, 0)

    if last:
        half = queries // 2
        for head in range(heads):
            j, h = head // 2, head % 2
            give_ref[head, 0 : HEAD + 8] = acc_ref[head, 0 : HEAD + 8, half:]
            give_ref[head, HEAD + 8 : HEAD + 16] = jnp.broadcast_to(
                max_ref[j, :, h * queries + half : (h + 1) * queries], (8, half)
            )


def join_kernel(acc_ref, max_ref, got_ref, wo_ref, out_ref):
    heads, _, queries = acc_ref.shape
    half = queries // 2
    parts = []
    for head in range(heads):
        j, h = head // 2, head % 2
        top = max_ref[j, :, h * queries : h * queries + half]
        other = got_ref[head, HEAD + 8 : HEAD + 9]
        both = jnp.maximum(top, other)
        mine, theirs = jnp.exp2(top - both), jnp.exp2(other - both)
        total = acc_ref[head, 0 : HEAD + 8, 0:half] * mine + got_ref[head, 0 : HEAD + 8] * theirs
        parts.append((total[:HEAD] / total[HEAD : HEAD + 1]).astype(BF16))
    attended = jnp.concatenate(parts, axis=0)
    out_ref[...] = lax.dot_general(attended, wo_ref[...], TN, preferred_element_type=F32).astype(
        BF16
    )


def shift_by(value, axis, step):
    count = lax.axis_size(axis)
    return lax.ppermute(value, axis, [(i, (i + step) % count) for i in range(count)])


def shards(
    latent, norm1_gain, norm1_shift, conv_weight, norm2_gain, norm2_shift,
    w_query, w_key, w_value, w_out,
):
    rows, cols, channels = latent.shape
    local = rows * cols
    heads = channels // HEAD
    pairs = heads // 2
    devices = math.prod(lax.axis_size(a) for a in PARTS)
    sds = jax.ShapeDtypeStruct
    vec = lambda v: v.reshape(1, channels)

    moments = pl.pallas_call(
        moments_kernel, out_shape=sds((devices, 2, channels), F32), compiler_params=params()
    )(latent)
    gathered = lax.all_to_all(moments, PARTS, 0, 0)

    def neighbours(low_edge, high_edge, axis):
        count = math.prod(lax.axis_size(a) for a in axis)
        forward = [(i, i + 1) for i in range(count - 1)]
        backward = [(b, a) for a, b in forward]
        return lax.ppermute(high_edge, axis, forward), lax.ppermute(low_edge, axis, backward)

    top, bot = neighbours(latent[:1], latent[-1:], ("row",))
    tall = lambda i: jnp.concatenate([top[:, i : i + 1], latent[:, i : i + 1], bot[:, i : i + 1]], 0)
    left, right = neighbours(tall(0), tall(cols - 1), ("x", "core"))
    row = lax.axis_index("row")
    col = lax.axis_index(("x", "core"))
    edges = jnp.stack(
        [row > 0, row < lax.axis_size("row") - 1, col > 0,
         col < lax.axis_size("x") * lax.axis_size("core") - 1]
    ).astype(jnp.int32)
    vm = pl.BlockSpec(memory_space=pltpu.VMEM)
    conv_update, stream, moments2 = pl.pallas_call(
        conv_kernel,
        in_specs=[pl.BlockSpec(memory_space=pltpu.SMEM)] + [vm] * 8
        + [pl.BlockSpec(memory_space=pl.ANY)],
        out_specs=[vm] * 3,
        out_shape=[
            sds((rows, cols, channels), BF16),
            sds((local, channels), BF16),
            sds((devices, 2, channels), F32),
        ],
        scratch_shapes=[
            pltpu.VMEM((9 * channels, channels), BF16), pltpu.SemaphoreType.DMA((3,))
        ],
        compiler_params=params(),
    )(
        edges, latent, top, bot, left, right, gathered, vec(norm1_gain), vec(norm1_shift),
        conv_weight.reshape(9 * channels, channels),
    )

    swap = lambda v: shift_by(v, "core", 1)
    cross = lambda v: shift_by(v, "x", 1)
    up = lambda v: shift_by(v, "row", 1)
    down = lambda v: shift_by(v, "row", -1)
    tie = lax.optimization_barrier
    own_peer = swap(stream)
    x0, ym, yp = cross(stream), up(stream), down(stream)
    gathered2 = lax.all_to_all(moments2, PARTS, 0, 0)
    x0, ym, yp, gathered2 = tie((x0, ym, yp, gathered2))
    xm, y2, xp = cross(ym), up(ym), down(x0)

    wqt, wvt = w_query.T, w_value.T
    state = [
        sds((heads, HEAD + 16, 2 * local), F32),
        sds((pairs, 1, 4 * local), F32),
    ]
    work = lambda count: [
        pltpu.VMEM((count * local, channels), BF16),
        pltpu.VMEM((channels, count * local), BF16),
    ]

    def cost(us):
        return pl.CostEstimate(flops=int(us * 1e9), bytes_accessed=0, transcendentals=0)

    affine, qbd, acc, top_scores = pl.pallas_call(
        first_kernel,
        out_shape=[sds((8, channels), F32), sds((pairs, 2 * HEAD, 4 * local), BF16)] + state,
        scratch_shapes=work(1),
        compiler_params=params(),
        cost_estimate=cost(5),
    )(stream, own_peer, gathered2, vec(norm2_gain), vec(norm2_shift), wqt, w_key, wvt)

    def more(blocks, acc, top_scores, last):
        return pl.pallas_call(
            lambda *refs: more_kernel(len(blocks), last, *refs),
            out_shape=state + [sds((heads, HEAD + 16, local), F32)] * last,
            scratch_shapes=work(len(blocks)),
            compiler_params=params(),
            cost_estimate=cost(3 * len(blocks)),
        )(*blocks, affine, qbd, acc, top_scores, w_key, wvt)

    acc, top_scores = more([x0, ym, yp], acc, top_scores, False)
    x2 = cross(y2)
    acc, top_scores = more([xm, y2, xp], acc, top_scores, False)
    acc, top_scores, give = more([x2], acc, top_scores, True)
    got = swap(give)
    attn = pl.pallas_call(
        join_kernel, out_shape=sds((local, channels), BF16), compiler_params=params()
    )(acc, top_scores, got, w_out)
    return conv_update, attn.reshape(rows, cols, channels)


def solution(mesh):
    sizes = dict(mesh.shape)
    split = Mesh(
        mesh.devices.reshape(sizes["batch"], sizes["row"], sizes["col"] // 2, 2),
        ("batch", "row", "x", "core"),
    )
    tiles = P(("batch", "row"), ("x", "core"), None)
    return jax.shard_map(
        shards,
        mesh=split,
        in_specs=(tiles,) + (P(),) * 9,
        out_specs=(tiles, tiles),
        check_vma=False,
    )
```

```python
import math

import jax
import jax.numpy as jnp
from jax import lax
from jax.experimental import pallas as pl
from jax.experimental.pallas import tpu as pltpu
from jax.sharding import Mesh
from jax.sharding import PartitionSpec as P

GROUPS = 32
HEAD = 64
EPS = 1e-05
F32 = jnp.float32
BF16 = jnp.bfloat16
NT = (((1,), (1,)), ((), ()))
TN = (((0,), (0,)), ((), ()))
PARTS = ("row", "x", "core")
LANES = 128
VMEM_LIMIT = 28 * 2**20
HEADROOM = 64.0


def cost(us):
    return pl.CostEstimate(flops=int(us * 1e9), bytes_accessed=0, transcendentals=0)


def params(limit=VMEM_LIMIT):
    return pltpu.CompilerParams(vmem_limit_bytes=limit)


def member(rows_are_channels, channels):
    per_group = channels // GROUPS
    shape = (channels, LANES) if rows_are_channels else (LANES, channels)
    channel = lax.broadcasted_iota(jnp.int32, shape, 0 if rows_are_channels else 1)
    group = lax.broadcasted_iota(jnp.int32, shape, 1 if rows_are_channels else 0)
    inside = (channel >= group * per_group) & (channel < (group + 1) * per_group)
    return jnp.where(inside, 1.0, 0.0).astype(BF16)


def planes_of(value):
    parts = []
    for _ in range(3):
        part = value.astype(BF16).astype(F32)
        parts.append(part)
        value = value - part
    return parts


def row_stack(rows, count):
    pad = [jnp.zeros((count - len(rows), rows[0].shape[1]), F32)] if len(rows) < count else []
    return jnp.concatenate(rows + pad, axis=0)


def through(vectors, one_hot):
    rows = [part for vector in vectors for part in planes_of(vector)]
    out = jnp.dot(row_stack(rows, 16).astype(BF16), one_hot, preferred_element_type=F32)
    return [
        out[3 * i : 3 * i + 1] + out[3 * i + 1 : 3 * i + 2] + out[3 * i + 2 : 3 * i + 3]
        for i in range(len(vectors))
    ]


def local_moments(values):
    mean = jnp.sum(values, axis=0, keepdims=True) * (1.0 / values.shape[0])
    off = values - mean
    return mean, jnp.sum(off * off, axis=0, keepdims=True)


def combine_moments(means, squares, local_pixels):
    devices, channels = means.shape
    per_group = channels // GROUPS
    pixels = devices * local_pixels
    mean_c = jnp.sum(means, axis=0, keepdims=True) * (1.0 / devices)
    off = means - mean_c
    square_c = jnp.sum(squares, axis=0, keepdims=True) + local_pixels * jnp.sum(
        off * off, axis=0, keepdims=True
    )
    to_group, to_channel = member(True, channels), member(False, channels)
    (sum_g,) = through([mean_c], to_group)
    (mean,) = through([sum_g * (1.0 / per_group)], to_channel)
    gap = mean_c - mean
    (square_g,) = through([square_c + pixels * (gap * gap)], to_group)
    inv = 1.0 / jnp.sqrt(square_g * (1.0 / (pixels * per_group)) + EPS)
    (inv,) = through([inv], to_channel)
    return mean, inv


def place():
    return lax.axis_index("row"), lax.axis_index("x") * lax.axis_size("core") + lax.axis_index("core")


AROUND = [(a, b) for a in (-1, 0, 1) for b in (-1, 0, 1) if (a, b) != (0, 0)]


def slot_of(grid_rows, grid_cols, a, b):
    row, col = place()
    inside = (row + a >= 0) & (row + a < grid_rows) & (col + b >= 0) & (col + b < grid_cols)
    return inside, jnp.where(inside, (row + a) * grid_cols + col + b, 0)


def edge_kernel(grid_rows, grid_cols, lat_ref, out_ref):
    rows, cols, channels = lat_ref.shape
    lat = lat_ref[...]
    mean, square = local_moments(lat.reshape(rows * cols, channels).astype(F32))
    table = row_stack(planes_of(mean) + planes_of(square), 8).astype(BF16)
    out_ref[:, rows:] = jnp.broadcast_to(table[None], (out_ref.shape[0], 8, channels))
    for a, b in AROUND:
        inside, slot = slot_of(grid_rows, grid_cols, a, b)

        @pl.when(inside)
        def _(a=a, b=b, slot=slot):
            line = 0 if a < 0 else rows - 1
            pixel = 0 if b < 0 else cols - 1
            if b == 0:
                edge = lat[line]
            elif a == 0:
                edge = lat[:, pixel]
            else:
                edge = jnp.broadcast_to(lat[line, pixel : pixel + 1], (rows, channels))
            out_ref[pl.ds(slot, 1), :rows] = edge[None]


def conv_kernel(
    grid_rows, grid_cols, lat_ref, near_ref, gain_ref, shift_ref, w_ref,
    conv_ref, stream_ref, out_stat_ref, pad_ref,
):
    rows, cols, channels = lat_ref.shape
    table = near_ref[:, rows:].astype(F32)
    means = table[:, 0] + table[:, 1] + table[:, 2]
    squares = table[:, 3] + table[:, 4] + table[:, 5]
    mean, inv = combine_moments(means, squares, rows * cols)
    scale = inv * gain_ref[...].reshape(1, channels)
    shift = shift_ref[...].reshape(1, channels)

    def act(raw):
        u = (raw.astype(F32) - mean) * scale + shift
        return u / (1.0 + jnp.exp(-u))

    base = 8
    flat = lat_ref[...].reshape(rows * cols, channels)
    pad_ref[1 : rows + 1, base : base + cols] = act(flat).reshape(rows, cols, channels)
    for a, b in AROUND:
        inside, slot = slot_of(grid_rows, grid_cols, a, b)
        values = jnp.where(inside, act(near_ref[slot, :rows]), 0.0)
        line = 0 if a < 0 else rows + 1
        pixel = base - 1 if b < 0 else base + cols
        if b == 0:
            pad_ref[line, base : base + cols] = values
        elif a == 0:
            for i in range(rows):
                pad_ref[1 + i, pixel : pixel + 1] = values[i : i + 1]
        else:
            pad_ref[line, pixel : pixel + 1] = values[0:1]
    shifted = [pad_ref[:, base + b - 1 : base + b - 1 + cols].astype(BF16) for b in range(3)]
    depth = 3 * channels
    total = None
    for t in range(3):
        window = jnp.concatenate(
            [s[t : t + rows].reshape(rows * cols, channels) for s in shifted], axis=1
        )
        part = jnp.dot(window, w_ref[pl.ds(t * depth, depth), :], preferred_element_type=F32)
        total = part if total is None else total + part
    update = total.astype(BF16)
    conv_ref[...] = update.reshape(rows, cols, channels)
    stream = (flat.astype(F32) + update.astype(F32)).astype(BF16)
    stream_ref[...] = stream
    mean, square = local_moments(stream.astype(F32))
    out_stat_ref[...] = jnp.broadcast_to(
        jnp.concatenate([mean, square], axis=0)[None], out_stat_ref.shape
    )


def normalise(block, affine):
    return ((block.astype(F32) - affine[0:1]) * affine[1:2] + affine[2:3]).astype(BF16)


def project(blocks, affine, wk_ref, wvt_ref, key_ref, value_ref, start=0):
    raw = jnp.concatenate(blocks, axis=0) if len(blocks) > 1 else blocks[0]
    normed = normalise(raw, affine)
    place = slice(start, start + raw.shape[0])
    key_ref[place] = jnp.dot(normed, wk_ref[...], preferred_element_type=F32).astype(BF16)
    value_ref[:, place] = lax.dot_general(
        wvt_ref[...], normed, NT, preferred_element_type=F32
    ).astype(BF16)


def stacked(values):
    return jnp.concatenate([values, jnp.ones((16, values.shape[1]), BF16)], axis=0)


def attend(low, top, key_ref, value_ref, qbd, put):
    scores = jnp.dot(key_ref[:, low : low + 2 * HEAD], qbd, preferred_element_type=F32)
    weights = jnp.exp2(scores - top).astype(BF16)
    queries = scores.shape[1] // 2
    for h in range(2):
        put(h, jnp.dot(
            stacked(value_ref[low + HEAD * h : low + HEAD * h + HEAD]),
            weights[:, h * queries : (h + 1) * queries],
            preferred_element_type=F32,
        ))
    return jnp.max(scores.reshape(-1, 8, 2 * queries), axis=0)


def attend_again(low, top, key_ref, value_ref, qbd, put):
    scores = jnp.dot(key_ref[:, pl.ds(low, 2 * HEAD)], qbd, preferred_element_type=F32)
    new = jnp.maximum(top, jnp.max(scores, axis=0, keepdims=True))
    weights = jnp.exp2(scores - new).astype(BF16)
    rescale = jnp.exp2(top - new)
    queries = scores.shape[1] // 2
    for h in range(2):
        side = slice(h * queries, (h + 1) * queries)
        put(h, rescale[:, side], jnp.dot(
            stacked(value_ref[pl.ds(low + HEAD * h, HEAD)]), weights[:, side],
            preferred_element_type=F32,
        ))
    return new


def fetch(sources, held_ref, sems):
    copies = [
        pltpu.make_async_copy(source, held_ref.at[i], sems.at[i])
        for i, source in enumerate(sources)
    ]
    for copy in copies:
        copy.start()
    return copies


def first_kernel(
    own_any, x0_any, ym_any, yp_any, peer_any, stat_ref, gain_ref, shift_ref, wqt_ref, wk_ref,
    wvt_ref, aff_ref, qbd_ref, acc_ref, max_ref, key_ref, value_ref, held_ref, sems,
):
    copies = fetch([own_any, peer_any, x0_any, ym_any, yp_any], held_ref, sems)
    _, length, channels = held_ref.shape
    pairs = channels // (2 * HEAD)
    queries = 2 * length
    stats = stat_ref[...]
    mean, inv = combine_moments(stats[:, 0], stats[:, 1], length)
    affine = row_stack(
        [mean, inv * gain_ref[...].reshape(1, channels), shift_ref[...].reshape(1, channels)], 8
    )
    aff_ref[...] = affine
    for copy in copies:
        copy.wait()
    own = held_ref[0]
    normed = normalise(jnp.concatenate([own, held_ref[1]], axis=0), affine)
    factor = math.log2(math.e) / math.sqrt(HEAD)
    qt = (
        lax.dot_general(wqt_ref[...], normed, NT, preferred_element_type=F32) * factor
    ).astype(BF16)
    zero = jnp.zeros((HEAD, queries), BF16)
    blocks = [own] + [held_ref[i] for i in range(2, 5)]
    project(blocks, affine, wk_ref, wvt_ref, key_ref, value_ref)
    for j in range(pairs):
        low = 2 * HEAD * j
        qbd = jnp.concatenate(
            [
                jnp.concatenate([qt[low : low + HEAD], zero], axis=1),
                jnp.concatenate([zero, qt[low + HEAD : low + 2 * HEAD]], axis=1),
            ],
            axis=0,
        )
        qbd_ref[j] = qbd
        few = jnp.dot(key_ref[0:LANES, low : low + 2 * HEAD], qbd, preferred_element_type=F32)
        max_ref[j] = jnp.max(few, axis=0, keepdims=True)
    excess = None
    for j in range(pairs):

        def put(h, value):
            acc_ref[2 * j + h] = value

        high = attend(2 * HEAD * j, max_ref[j], key_ref, value_ref, qbd_ref[j], put)
        over = high - max_ref[j]
        excess = over if excess is None else jnp.maximum(excess, over)

    @pl.when(jnp.max(excess) > HEADROOM)
    def _():
        def one_pair(j, _):
            def put(h, rescale, value):
                acc_ref[2 * j + h] = value

            low = pl.multiple_of(2 * HEAD * j, 2 * HEAD)
            max_ref[j] = attend_again(low, max_ref[j], key_ref, value_ref, qbd_ref[j], put)
            return 0

        lax.fori_loop(0, pairs, one_pair, 0)


def more_kernel(count, last, *refs):
    near, far_any = refs[: count - 1], refs[count - 1]
    aff_ref, qbd_ref, acc_in, max_in, wk_ref, wvt_ref, acc_ref, max_ref = refs[count : count + 8]
    if last:
        give_ref, key_ref, value_ref, held_ref, sems = refs[count + 8 :]
    else:
        key_ref, value_ref, held_ref, sems = refs[count + 8 :]
    copies = fetch([far_any], held_ref, sems)
    heads, _, queries = acc_in.shape
    pairs = heads // 2
    work = (aff_ref[...], wk_ref, wvt_ref, key_ref, value_ref)
    project([b[...] for b in near], *work)
    copies[0].wait()
    project([held_ref[0]], *work, start=(count - 1) * held_ref.shape[1])
    excess = None
    for j in range(pairs):

        def put(h, value):
            acc_ref[2 * j + h] = acc_in[2 * j + h] + value

        high = attend(2 * HEAD * j, max_in[j], key_ref, value_ref, qbd_ref[j], put)
        over = high - max_in[j]
        excess = over if excess is None else jnp.maximum(excess, over)
    max_ref[...] = max_in[...]

    @pl.when(jnp.max(excess) > HEADROOM)
    def _():
        def one_pair(j, _):
            def put(h, rescale, value):
                acc_ref[2 * j + h] = acc_in[2 * j + h] * rescale + value

            low = pl.multiple_of(2 * HEAD * j, 2 * HEAD)
            max_ref[j] = attend_again(low, max_in[j], key_ref, value_ref, qbd_ref[j], put)
            return 0

        lax.fori_loop(0, pairs, one_pair, 0)

    if last:
        half = queries // 2
        logs = []
        for head in range(heads):
            j, h = head // 2, head % 2
            total = acc_ref[head, HEAD : HEAD + 1, half:]
            give_ref[HEAD * head : HEAD * head + HEAD] = (
                acc_ref[head, 0:HEAD, half:] / total
            ).astype(BF16)
            logs.append(
                max_ref[j, :, h * queries + half : (h + 1) * queries]
                + jnp.log(total) * math.log2(math.e)
            )
        value = jnp.concatenate(logs + [jnp.zeros((16 - heads, half), F32)], axis=0)
        base = HEAD * heads
        for i in range(3):
            part = value.astype(BF16)
            give_ref[base + 16 * i : base + 16 * i + 16] = part
            value = value - part.astype(F32)


def join_kernel(acc_ref, max_ref, got_ref, wo_ref, out_ref):
    heads, _, queries = acc_ref.shape
    half = queries // 2
    base = HEAD * heads
    logs = sum(got_ref[base + 16 * i : base + 16 * i + 16].astype(F32) for i in range(3))
    parts = []
    for head in range(heads):
        j, h = head // 2, head % 2
        top = max_ref[j, :, h * queries : h * queries + half]
        other = logs[head : head + 1]
        both = jnp.maximum(top, other)
        mine, theirs = jnp.exp2(top - both), jnp.exp2(other - both)
        total = acc_ref[head, HEAD : HEAD + 1, 0:half] * mine + theirs
        inverse = 1.0 / total
        found = got_ref[HEAD * head : HEAD * head + HEAD].astype(F32)
        parts.append(
            (acc_ref[head, 0:HEAD, 0:half] * (mine * inverse) + found * (theirs * inverse)).astype(
                BF16
            )
        )
    attended = jnp.concatenate(parts, axis=0)
    out_ref[...] = lax.dot_general(attended, wo_ref[...], TN, preferred_element_type=F32).astype(
        BF16
    )


def shift_by(value, axis, step):
    count = lax.axis_size(axis)
    return lax.ppermute(value, axis, [(i, (i + step) % count) for i in range(count)])


def shards(
    latent, norm1_gain, norm1_shift, conv_weight, norm2_gain, norm2_shift,
    w_query, w_key, w_value, w_out,
):
    rows, cols, channels = latent.shape
    local = rows * cols
    heads = channels // HEAD
    pairs = heads // 2
    devices = math.prod(lax.axis_size(a) for a in PARTS)
    sds = jax.ShapeDtypeStruct
    grid = (lax.axis_size("row"), lax.axis_size("x") * lax.axis_size("core"))
    vm = pl.BlockSpec(memory_space=pltpu.VMEM)

    tie = lax.optimization_barrier
    slots = pl.pallas_call(
        lambda *refs: edge_kernel(*grid, *refs),
        in_specs=[vm],
        out_specs=vm,
        out_shape=sds((devices, rows + 8, channels), BF16),
        cost_estimate=cost(2),
        compiler_params=params(8 * 2**20),
    )(latent)
    near = lax.all_to_all(slots, PARTS, 0, 0)
    near, wqt, wvt = tie((near, w_query.T, w_value.T))
    conv_update, stream, moments2 = pl.pallas_call(
        lambda *refs: conv_kernel(*grid, *refs),
        in_specs=[vm] * 5,
        out_specs=[vm] * 3,
        out_shape=[
            sds((rows, cols, channels), BF16),
            sds((local, channels), BF16),
            sds((devices, 2, channels), F32),
        ],
        scratch_shapes=[pltpu.VMEM((rows + 2, cols + 16, channels), F32)],
        cost_estimate=cost(5),
        compiler_params=params(),
    )(latent, near, norm1_gain, norm1_shift, conv_weight.reshape(9 * channels, channels))

    swap = lambda v: shift_by(v, "core", 1)
    cross = lambda v: shift_by(v, "x", 1)
    up = lambda v: shift_by(v, "row", 1)
    down = lambda v: shift_by(v, "row", -1)
    own_peer = swap(stream)
    x0, ym, yp = cross(stream), up(stream), down(stream)
    gathered2 = lax.all_to_all(moments2, PARTS, 0, 0)
    span = lax.axis_size("row")
    far = [
        (2 * y + x, 2 * ((y + span // 2) % span) + 1 - x) for y in range(span) for x in range(2)
    ]
    x2 = lax.ppermute(stream, ("row", "x"), far)
    x0, ym, yp, gathered2 = tie((x0, ym, yp, gathered2))
    xm, y2, xp = cross(ym), up(ym), down(x0)

    state = [
        sds((heads, HEAD + 16, 2 * local), F32),
        sds((pairs, 1, 4 * local), F32),
    ]
    work = lambda keys, blocks: [
        pltpu.VMEM((keys * local, channels), BF16),
        pltpu.VMEM((channels, keys * local), BF16),
        pltpu.VMEM((blocks, local, channels), BF16),
        pltpu.SemaphoreType.DMA((blocks,)),
    ]
    anywhere = pl.BlockSpec(memory_space=pl.ANY)

    affine, qbd, acc, top_scores = pl.pallas_call(
        first_kernel,
        out_shape=[sds((8, channels), F32), sds((pairs, 2 * HEAD, 4 * local), BF16)] + state,
        in_specs=[anywhere] * 5 + [vm] * 6,
        scratch_shapes=work(4, 5),
        compiler_params=params(),
        cost_estimate=cost(9),
    )(stream, x0, ym, yp, own_peer, gathered2, norm2_gain, norm2_shift, wqt, w_key, wvt)

    def more(blocks, acc, top_scores, last):
        count = len(blocks)
        return pl.pallas_call(
            lambda *refs: more_kernel(len(blocks), last, *refs),
            out_shape=state + [sds((channels + 3 * 16, local), BF16)] * last,
            in_specs=[vm] * (count - 1) + [anywhere] + [vm] * 6,
            scratch_shapes=work(count, 1),
            compiler_params=params(),
            cost_estimate=cost(2 * count),
        )(*blocks, affine, qbd, acc, top_scores, w_key, wvt)

    acc, top_scores, give = more([xm, y2, xp, x2], acc, top_scores, True)
    got = swap(give)
    attn = pl.pallas_call(
        join_kernel, out_shape=sds((local, channels), BF16), compiler_params=params()
    )(acc, top_scores, got, w_out)
    return conv_update, attn.reshape(rows, cols, channels)


def solution(mesh):
    sizes = dict(mesh.shape)
    split = Mesh(
        mesh.devices.reshape(sizes["batch"], sizes["row"], sizes["col"] // 2, 2),
        ("batch", "row", "x", "core"),
    )
    tiles = P(("batch", "row"), ("x", "core"), None)
    return jax.shard_map(
        shards,
        mesh=split,
        in_specs=(tiles,) + (P(),) * 9,
        out_specs=(tiles, tiles),
        check_vma=False,
    )
```

```python
import math

import jax
import jax.numpy as jnp
from jax import lax
from jax.experimental import pallas as pl
from jax.experimental.pallas import tpu as pltpu
from jax.sharding import Mesh
from jax.sharding import PartitionSpec as P

GROUPS = 32
HEAD = 64
EPS = 1e-05
F32 = jnp.float32
BF16 = jnp.bfloat16
NT = (((1,), (1,)), ((), ()))
TN = (((0,), (0,)), ((), ()))
PARTS = ("row", "x", "core")
LANES = 128
VMEM_LIMIT = 28 * 2**20
HEADROOM = 64.0


def cost(us):
    return pl.CostEstimate(flops=int(us * 1e9), bytes_accessed=0, transcendentals=0)


def params(limit=VMEM_LIMIT):
    return pltpu.CompilerParams(vmem_limit_bytes=limit)


def member(rows_are_channels, channels):
    per_group = channels // GROUPS
    shape = (channels, LANES) if rows_are_channels else (LANES, channels)
    channel = lax.broadcasted_iota(jnp.int32, shape, 0 if rows_are_channels else 1)
    group = lax.broadcasted_iota(jnp.int32, shape, 1 if rows_are_channels else 0)
    inside = (channel >= group * per_group) & (channel < (group + 1) * per_group)
    return jnp.where(inside, 1.0, 0.0).astype(BF16)


def planes_of(value):
    parts = []
    for _ in range(3):
        part = value.astype(BF16).astype(F32)
        parts.append(part)
        value = value - part
    return parts


def row_stack(rows, count):
    pad = [jnp.zeros((count - len(rows), rows[0].shape[1]), F32)] if len(rows) < count else []
    return jnp.concatenate(rows + pad, axis=0)


def through(vectors, one_hot):
    rows = [part for vector in vectors for part in planes_of(vector)]
    out = jnp.dot(row_stack(rows, 16).astype(BF16), one_hot, preferred_element_type=F32)
    return [
        out[3 * i : 3 * i + 1] + out[3 * i + 1 : 3 * i + 2] + out[3 * i + 2 : 3 * i + 3]
        for i in range(len(vectors))
    ]


def local_moments(values):
    mean = jnp.sum(values, axis=0, keepdims=True) * (1.0 / values.shape[0])
    off = values - mean
    return mean, jnp.sum(off * off, axis=0, keepdims=True)


def combine_moments(means, squares, local_pixels):
    devices, channels = means.shape
    per_group = channels // GROUPS
    pixels = devices * local_pixels
    mean_c = jnp.sum(means, axis=0, keepdims=True) * (1.0 / devices)
    off = means - mean_c
    square_c = jnp.sum(squares, axis=0, keepdims=True) + local_pixels * jnp.sum(
        off * off, axis=0, keepdims=True
    )
    to_group, to_channel = member(True, channels), member(False, channels)
    (sum_g,) = through([mean_c], to_group)
    (mean,) = through([sum_g * (1.0 / per_group)], to_channel)
    gap = mean_c - mean
    (square_g,) = through([square_c + pixels * (gap * gap)], to_group)
    inv = 1.0 / jnp.sqrt(square_g * (1.0 / (pixels * per_group)) + EPS)
    (inv,) = through([inv], to_channel)
    return mean, inv


def place():
    return lax.axis_index("row"), lax.axis_index("x") * lax.axis_size("core") + lax.axis_index("core")


AROUND = [(a, b) for a in (-1, 0, 1) for b in (-1, 0, 1) if (a, b) != (0, 0)]


def slot_of(grid_rows, grid_cols, a, b):
    row, col = place()
    inside = (row + a >= 0) & (row + a < grid_rows) & (col + b >= 0) & (col + b < grid_cols)
    return inside, jnp.where(inside, (row + a) * grid_cols + col + b, 0)


def edge_kernel(grid_rows, grid_cols, lat_ref, out_ref):
    rows, cols, channels = lat_ref.shape
    lat = lat_ref[...]
    mean, square = local_moments(lat.reshape(rows * cols, channels).astype(F32))
    table = row_stack(planes_of(mean) + planes_of(square), 8).astype(BF16)
    out_ref[:, rows:] = jnp.broadcast_to(table[None], (out_ref.shape[0], 8, channels))
    for a, b in AROUND:
        inside, slot = slot_of(grid_rows, grid_cols, a, b)

        @pl.when(inside)
        def _(a=a, b=b, slot=slot):
            line = 0 if a < 0 else rows - 1
            pixel = 0 if b < 0 else cols - 1
            if b == 0:
                edge = lat[line]
            elif a == 0:
                edge = lat[:, pixel]
            else:
                edge = jnp.broadcast_to(lat[line, pixel : pixel + 1], (rows, channels))
            out_ref[pl.ds(slot, 1), :rows] = edge[None]


def conv_kernel(
    grid_rows, grid_cols, lat_ref, near_ref, gain_ref, shift_ref, w_ref,
    conv_ref, stream_ref, out_stat_ref, pad_ref,
):
    rows, cols, channels = lat_ref.shape
    table = near_ref[:, rows:].astype(F32)
    means = table[:, 0] + table[:, 1] + table[:, 2]
    squares = table[:, 3] + table[:, 4] + table[:, 5]
    mean, inv = combine_moments(means, squares, rows * cols)
    scale = inv * gain_ref[...].reshape(1, channels)
    shift = shift_ref[...].reshape(1, channels)

    def act(raw):
        u = (raw.astype(F32) - mean) * scale + shift
        return u / (1.0 + jnp.exp(-u))

    base = 8
    flat = lat_ref[...].reshape(rows * cols, channels)
    pad_ref[1 : rows + 1, base : base + cols] = act(flat).reshape(rows, cols, channels)
    for a, b in AROUND:
        inside, slot = slot_of(grid_rows, grid_cols, a, b)
        values = jnp.where(inside, act(near_ref[slot, :rows]), 0.0)
        line = 0 if a < 0 else rows + 1
        pixel = base - 1 if b < 0 else base + cols
        if b == 0:
            pad_ref[line, base : base + cols] = values
        elif a == 0:
            for i in range(rows):
                pad_ref[1 + i, pixel : pixel + 1] = values[i : i + 1]
        else:
            pad_ref[line, pixel : pixel + 1] = values[0:1]
    shifted = [pad_ref[:, base + b - 1 : base + b - 1 + cols].astype(BF16) for b in range(3)]
    depth = 3 * channels
    total = None
    for t in range(3):
        window = jnp.concatenate(
            [s[t : t + rows].reshape(rows * cols, channels) for s in shifted], axis=1
        )
        part = jnp.dot(window, w_ref[pl.ds(t * depth, depth), :], preferred_element_type=F32)
        total = part if total is None else total + part
    update = total.astype(BF16)
    conv_ref[...] = update.reshape(rows, cols, channels)
    stream = (flat.astype(F32) + update.astype(F32)).astype(BF16)
    stream_ref[...] = stream
    mean, square = local_moments(stream.astype(F32))
    out_stat_ref[...] = jnp.broadcast_to(
        jnp.concatenate([mean, square], axis=0)[None], out_stat_ref.shape
    )


def normalise(block, affine):
    return ((block.astype(F32) - affine[0:1]) * affine[1:2] + affine[2:3]).astype(BF16)


def project(blocks, affine, wk_ref, wvt_ref, key_ref, value_ref, start=0):
    raw = jnp.concatenate(blocks, axis=0) if len(blocks) > 1 else blocks[0]
    normed = normalise(raw, affine)
    place = slice(start, start + raw.shape[0])
    key_ref[place] = jnp.dot(normed, wk_ref[...], preferred_element_type=F32).astype(BF16)
    value_ref[:, place] = lax.dot_general(
        wvt_ref[...], normed, NT, preferred_element_type=F32
    ).astype(BF16)


def stacked(values):
    return jnp.concatenate([values, jnp.ones((16, values.shape[1]), BF16)], axis=0)


def attend(low, top, key_ref, value_ref, qbd, put):
    scores = jnp.dot(key_ref[:, low : low + 2 * HEAD], qbd, preferred_element_type=F32)
    weights = jnp.exp2(scores - top).astype(BF16)
    queries = scores.shape[1] // 2
    for h in range(2):
        put(h, jnp.dot(
            stacked(value_ref[low + HEAD * h : low + HEAD * h + HEAD]),
            weights[:, h * queries : (h + 1) * queries],
            preferred_element_type=F32,
        ))
    return jnp.max(scores.reshape(-1, 8, 2 * queries), axis=0)


def attend_again(low, top, key_ref, value_ref, qbd, put):
    scores = jnp.dot(key_ref[:, pl.ds(low, 2 * HEAD)], qbd, preferred_element_type=F32)
    new = jnp.maximum(top, jnp.max(scores, axis=0, keepdims=True))
    weights = jnp.exp2(scores - new).astype(BF16)
    rescale = jnp.exp2(top - new)
    queries = scores.shape[1] // 2
    for h in range(2):
        side = slice(h * queries, (h + 1) * queries)
        put(h, rescale[:, side], jnp.dot(
            stacked(value_ref[pl.ds(low + HEAD * h, HEAD)]), weights[:, side],
            preferred_element_type=F32,
        ))
    return new


def fetch(sources, held_ref, sems):
    copies = [
        pltpu.make_async_copy(source, held_ref.at[i], sems.at[i])
        for i, source in enumerate(sources)
    ]
    for copy in copies:
        copy.start()
    return copies


def first_kernel(
    own_any, x0_any, yp_any, peer_any, stat_ref, gain_ref, shift_ref, wqt_ref, wk_ref,
    wvt_ref, aff_ref, qbd_ref, acc_ref, max_ref, key_ref, value_ref, held_ref, sems,
):
    copies = fetch([own_any, peer_any, x0_any, yp_any], held_ref, sems)
    _, length, channels = held_ref.shape
    pairs = channels // (2 * HEAD)
    queries = 2 * length
    stats = stat_ref[...]
    mean, inv = combine_moments(stats[:, 0], stats[:, 1], length)
    affine = row_stack(
        [mean, inv * gain_ref[...].reshape(1, channels), shift_ref[...].reshape(1, channels)], 8
    )
    aff_ref[...] = affine
    for copy in copies:
        copy.wait()
    own = held_ref[0]
    normed = normalise(jnp.concatenate([own, held_ref[1]], axis=0), affine)
    factor = math.log2(math.e) / math.sqrt(HEAD)
    qt = (
        lax.dot_general(wqt_ref[...], normed, NT, preferred_element_type=F32) * factor
    ).astype(BF16)
    zero = jnp.zeros((HEAD, queries), BF16)
    blocks = [own] + [held_ref[i] for i in range(2, 4)]
    project(blocks, affine, wk_ref, wvt_ref, key_ref, value_ref)
    for j in range(pairs):
        low = 2 * HEAD * j
        qbd = jnp.concatenate(
            [
                jnp.concatenate([qt[low : low + HEAD], zero], axis=1),
                jnp.concatenate([zero, qt[low + HEAD : low + 2 * HEAD]], axis=1),
            ],
            axis=0,
        )
        qbd_ref[j] = qbd
        few = jnp.dot(key_ref[0:LANES, low : low + 2 * HEAD], qbd, preferred_element_type=F32)
        max_ref[j] = jnp.max(few, axis=0, keepdims=True)
    excess = None
    for j in range(pairs):

        def put(h, value):
            acc_ref[2 * j + h] = value

        high = attend(2 * HEAD * j, max_ref[j], key_ref, value_ref, qbd_ref[j], put)
        over = high - max_ref[j]
        excess = over if excess is None else jnp.maximum(excess, over)

    @pl.when(jnp.max(excess) > HEADROOM)
    def _():
        def one_pair(j, _):
            def put(h, rescale, value):
                acc_ref[2 * j + h] = value

            low = pl.multiple_of(2 * HEAD * j, 2 * HEAD)
            max_ref[j] = attend_again(low, max_ref[j], key_ref, value_ref, qbd_ref[j], put)
            return 0

        lax.fori_loop(0, pairs, one_pair, 0)


def more_kernel(head, tail, last, *refs):
    count = head + tail
    here, elsewhere = refs[:head], refs[head:count]
    aff_ref, qbd_ref, acc_in, max_in, wk_ref, wvt_ref, acc_ref, max_ref = refs[count : count + 8]
    give_ref, (key_ref, value_ref, *own) = refs[count + 8], refs[count + 8 + last :]
    copies = fetch(elsewhere, *own) if tail else []
    heads, _, queries = acc_in.shape
    pairs = heads // 2
    work = (aff_ref[...], wk_ref, wvt_ref, key_ref, value_ref)
    project([b[...] for b in here], *work)
    for copy in copies:
        copy.wait()
    if tail:
        held_ref = own[0]
        project([held_ref[i] for i in range(tail)], *work, start=head * held_ref.shape[1])
    excess = None
    for j in range(pairs):

        def put(h, value):
            acc_ref[2 * j + h] = acc_in[2 * j + h] + value

        high = attend(2 * HEAD * j, max_in[j], key_ref, value_ref, qbd_ref[j], put)
        over = high - max_in[j]
        excess = over if excess is None else jnp.maximum(excess, over)
    max_ref[...] = max_in[...]

    @pl.when(jnp.max(excess) > HEADROOM)
    def _():
        def one_pair(j, _):
            def put(h, rescale, value):
                acc_ref[2 * j + h] = acc_in[2 * j + h] * rescale + value

            low = pl.multiple_of(2 * HEAD * j, 2 * HEAD)
            max_ref[j] = attend_again(low, max_in[j], key_ref, value_ref, qbd_ref[j], put)
            return 0

        lax.fori_loop(0, pairs, one_pair, 0)

    if last:
        half = queries // 2
        logs = []
        for head in range(heads):
            j, h = head // 2, head % 2
            total = acc_ref[head, HEAD : HEAD + 1, half:]
            give_ref[HEAD * head : HEAD * head + HEAD] = (
                acc_ref[head, 0:HEAD, half:] / total
            ).astype(BF16)
            logs.append(
                max_ref[j, :, h * queries + half : (h + 1) * queries]
                + jnp.log(total) * math.log2(math.e)
            )
        value = jnp.concatenate(logs + [jnp.zeros((16 - heads, half), F32)], axis=0)
        base = HEAD * heads
        for i in range(3):
            part = value.astype(BF16)
            give_ref[base + 16 * i : base + 16 * i + 16] = part
            value = value - part.astype(F32)


def join_kernel(acc_ref, max_ref, got_ref, wo_ref, out_ref):
    heads, _, queries = acc_ref.shape
    half = queries // 2
    base = HEAD * heads
    logs = sum(got_ref[base + 16 * i : base + 16 * i + 16].astype(F32) for i in range(3))
    parts = []
    for head in range(heads):
        j, h = head // 2, head % 2
        top = max_ref[j, :, h * queries : h * queries + half]
        other = logs[head : head + 1]
        both = jnp.maximum(top, other)
        mine, theirs = jnp.exp2(top - both), jnp.exp2(other - both)
        total = acc_ref[head, HEAD : HEAD + 1, 0:half] * mine + theirs
        inverse = 1.0 / total
        found = got_ref[HEAD * head : HEAD * head + HEAD].astype(F32)
        parts.append(
            (acc_ref[head, 0:HEAD, 0:half] * (mine * inverse) + found * (theirs * inverse)).astype(
                BF16
            )
        )
    attended = jnp.concatenate(parts, axis=0)
    out_ref[...] = lax.dot_general(attended, wo_ref[...], TN, preferred_element_type=F32).astype(
        BF16
    )


def shift_by(value, axis, step):
    count = lax.axis_size(axis)
    return lax.ppermute(value, axis, [(i, (i + step) % count) for i in range(count)])


def shards(
    latent, norm1_gain, norm1_shift, conv_weight, norm2_gain, norm2_shift,
    w_query, w_key, w_value, w_out,
):
    rows, cols, channels = latent.shape
    local = rows * cols
    heads = channels // HEAD
    pairs = heads // 2
    devices = math.prod(lax.axis_size(a) for a in PARTS)
    sds = jax.ShapeDtypeStruct
    grid = (lax.axis_size("row"), lax.axis_size("x") * lax.axis_size("core"))
    vm = pl.BlockSpec(memory_space=pltpu.VMEM)

    tie = lax.optimization_barrier
    slots = pl.pallas_call(
        lambda *refs: edge_kernel(*grid, *refs),
        in_specs=[vm],
        out_specs=vm,
        out_shape=sds((devices, rows + 8, channels), BF16),
        cost_estimate=cost(2),
        compiler_params=params(8 * 2**20),
    )(latent)
    near = lax.all_to_all(slots, PARTS, 0, 0)
    near, wqt, wvt = tie((near, w_query.T, w_value.T))
    conv_update, stream, moments2 = pl.pallas_call(
        lambda *refs: conv_kernel(*grid, *refs),
        in_specs=[vm] * 5,
        out_specs=[vm] * 3,
        out_shape=[
            sds((rows, cols, channels), BF16),
            sds((local, channels), BF16),
            sds((devices, 2, channels), F32),
        ],
        scratch_shapes=[pltpu.VMEM((rows + 2, cols + 16, channels), F32)],
        cost_estimate=cost(5),
        compiler_params=params(),
    )(latent, near, norm1_gain, norm1_shift, conv_weight.reshape(9 * channels, channels))

    swap = lambda v: shift_by(v, "core", 1)
    cross = lambda v: shift_by(v, "x", 1)
    up = lambda v: shift_by(v, "row", 1)
    down = lambda v: shift_by(v, "row", -1)
    own_peer = swap(stream)
    x0, ym, yp = cross(stream), up(stream), down(stream)
    gathered2 = lax.all_to_all(moments2, PARTS, 0, 0)
    span = lax.axis_size("row")
    far = [
        (2 * y + x, 2 * ((y + span // 2) % span) + 1 - x) for y in range(span) for x in range(2)
    ]
    x2 = lax.ppermute(stream, ("row", "x"), far)
    xm, y2, xp = cross(ym), up(ym), down(x0)

    state = [
        sds((heads, HEAD + 16, 2 * local), F32),
        sds((pairs, 1, 4 * local), F32),
    ]
    work = lambda keys, blocks: [
        pltpu.VMEM((keys * local, channels), BF16),
        pltpu.VMEM((channels, keys * local), BF16),
        pltpu.VMEM((blocks, local, channels), BF16),
        pltpu.SemaphoreType.DMA((blocks,)),
    ]
    anywhere = pl.BlockSpec(memory_space=pl.ANY)

    affine, qbd, acc, top_scores = pl.pallas_call(
        first_kernel,
        out_shape=[sds((8, channels), F32), sds((pairs, 2 * HEAD, 4 * local), BF16)] + state,
        in_specs=[anywhere] * 4 + [vm] * 6,
        scratch_shapes=work(3, 4),
        compiler_params=params(),
        cost_estimate=cost(9),
    )(stream, x0, yp, own_peer, gathered2, norm2_gain, norm2_shift, wqt, w_key, wvt)

    def more(here, elsewhere, acc, top_scores, last):
        head, tail = len(here), len(elsewhere)
        count = head + tail
        return pl.pallas_call(
            lambda *refs: more_kernel(head, tail, last, *refs),
            out_shape=state + [sds((channels + 3 * 16, local), BF16)] * last,
            in_specs=[vm] * head + [anywhere] * tail + [vm] * 6,
            scratch_shapes=work(count, tail) if tail else work(count, 1)[:2],
            compiler_params=params(),
            cost_estimate=cost(2 * count),
        )(*here, *elsewhere, affine, qbd, acc, top_scores, w_key, wvt)

    acc, top_scores = more([ym], [x2], acc, top_scores, False)
    acc, top_scores, give = more([xm, xp, y2], [], acc, top_scores, True)
    got = swap(give)
    attn = pl.pallas_call(
        join_kernel, out_shape=sds((local, channels), BF16), compiler_params=params()
    )(acc, top_scores, got, w_out)
    return conv_update, attn.reshape(rows, cols, channels)


def solution(mesh):
    sizes = dict(mesh.shape)
    split = Mesh(
        mesh.devices.reshape(sizes["batch"], sizes["row"], sizes["col"] // 2, 2),
        ("batch", "row", "x", "core"),
    )
    tiles = P(("batch", "row"), ("x", "core"), None)
    return jax.shard_map(
        shards,
        mesh=split,
        in_specs=(tiles,) + (P(),) * 9,
        out_specs=(tiles, tiles),
        check_vma=False,
    )
```

```python
import math

import jax
import jax.numpy as jnp
from jax import lax
from jax.experimental import pallas as pl
from jax.experimental.pallas import tpu as pltpu
from jax.sharding import Mesh
from jax.sharding import PartitionSpec as P

GROUPS = 32
HEAD = 64
EPS = 1e-05
F32 = jnp.float32
BF16 = jnp.bfloat16
NT = (((1,), (1,)), ((), ()))
TN = (((0,), (0,)), ((), ()))
PARTS = ("row", "x", "core")
LANES = 128
VMEM_LIMIT = 28 * 2**20
HEADROOM = 64.0


def cost(us):
    return pl.CostEstimate(flops=int(us * 1e9), bytes_accessed=0, transcendentals=0)


def params(limit=VMEM_LIMIT):
    return pltpu.CompilerParams(vmem_limit_bytes=limit)


def member(rows_are_channels, channels):
    per_group = channels // GROUPS
    shape = (channels, LANES) if rows_are_channels else (LANES, channels)
    channel = lax.broadcasted_iota(jnp.int32, shape, 0 if rows_are_channels else 1)
    group = lax.broadcasted_iota(jnp.int32, shape, 1 if rows_are_channels else 0)
    inside = (channel >= group * per_group) & (channel < (group + 1) * per_group)
    return jnp.where(inside, 1.0, 0.0).astype(BF16)


def planes_of(value):
    parts = []
    for _ in range(3):
        part = value.astype(BF16).astype(F32)
        parts.append(part)
        value = value - part
    return parts


def row_stack(rows, count):
    pad = [jnp.zeros((count - len(rows), rows[0].shape[1]), F32)] if len(rows) < count else []
    return jnp.concatenate(rows + pad, axis=0)


def through(vectors, one_hot):
    rows = [part for vector in vectors for part in planes_of(vector)]
    out = jnp.dot(row_stack(rows, 16).astype(BF16), one_hot, preferred_element_type=F32)
    return [
        out[3 * i : 3 * i + 1] + out[3 * i + 1 : 3 * i + 2] + out[3 * i + 2 : 3 * i + 3]
        for i in range(len(vectors))
    ]


def local_moments(values):
    mean = jnp.sum(values, axis=0, keepdims=True) * (1.0 / values.shape[0])
    off = values - mean
    return mean, jnp.sum(off * off, axis=0, keepdims=True)


def combine_moments(means, squares, local_pixels):
    devices, channels = means.shape
    per_group = channels // GROUPS
    pixels = devices * local_pixels
    mean_c = jnp.sum(means, axis=0, keepdims=True) * (1.0 / devices)
    off = means - mean_c
    square_c = jnp.sum(squares, axis=0, keepdims=True) + local_pixels * jnp.sum(
        off * off, axis=0, keepdims=True
    )
    to_group, to_channel = member(True, channels), member(False, channels)
    (sum_g,) = through([mean_c], to_group)
    (mean,) = through([sum_g * (1.0 / per_group)], to_channel)
    gap = mean_c - mean
    (square_g,) = through([square_c + pixels * (gap * gap)], to_group)
    inv = 1.0 / jnp.sqrt(square_g * (1.0 / (pixels * per_group)) + EPS)
    (inv,) = through([inv], to_channel)
    return mean, inv


def group_moments(values):
    count, channels = values.shape
    mean_c, square_c = local_moments(values)
    to_group, to_channel = member(True, channels), member(False, channels)
    sum_g, square_g = through([mean_c, square_c], to_group)
    mean_g = sum_g * (GROUPS / channels)
    (wide,) = through([mean_g], to_channel)
    gap = mean_c - wide
    (spread,) = through([gap * gap], to_group)
    return mean_g, square_g + count * spread


def combine_groups(means, squares, local_pixels, channels):
    devices = means.shape[0]
    count = local_pixels * (channels // GROUPS)
    mean = jnp.sum(means, axis=0, keepdims=True) * (1.0 / devices)
    off = means - mean
    square = jnp.sum(squares, axis=0, keepdims=True) + count * jnp.sum(
        off * off, axis=0, keepdims=True
    )
    inv = 1.0 / jnp.sqrt(square * (1.0 / (devices * count)) + EPS)
    return through([mean, inv], member(False, channels))


def place():
    return lax.axis_index("row"), lax.axis_index("x") * lax.axis_size("core") + lax.axis_index("core")


AROUND = [(a, b) for a in (-1, 0, 1) for b in (-1, 0, 1) if (a, b) != (0, 0)]


def slot_of(grid_rows, grid_cols, a, b):
    row, col = place()
    inside = (row + a >= 0) & (row + a < grid_rows) & (col + b >= 0) & (col + b < grid_cols)
    return inside, jnp.where(inside, (row + a) * grid_cols + col + b, 0)


def edge_kernel(grid_rows, grid_cols, lat_ref, out_ref):
    rows, cols, channels = lat_ref.shape
    lat = lat_ref[...]
    mean, square = group_moments(lat.reshape(rows * cols, channels).astype(F32))
    table = row_stack(planes_of(mean) + planes_of(square), rows).astype(BF16)
    out_ref[:, :, channels:] = jnp.broadcast_to(table[None], (out_ref.shape[0], rows, LANES))
    for a, b in AROUND:
        inside, slot = slot_of(grid_rows, grid_cols, a, b)

        @pl.when(inside)
        def _(a=a, b=b, slot=slot):
            line = 0 if a < 0 else rows - 1
            pixel = 0 if b < 0 else cols - 1
            if b == 0:
                edge = lat[line]
            elif a == 0:
                edge = lat[:, pixel]
            else:
                edge = jnp.broadcast_to(lat[line, pixel : pixel + 1], (rows, channels))
            out_ref[pl.ds(slot, 1), :, :channels] = edge[None]


def conv_kernel(
    grid_rows, grid_cols, lat_ref, near_ref, gain_ref, shift_ref, w_ref,
    conv_ref, stream_ref, out_stat_ref, pad_ref,
):
    rows, cols, channels = lat_ref.shape
    table = near_ref[:, :, channels:].astype(F32)
    means = table[:, 0] + table[:, 1] + table[:, 2]
    squares = table[:, 3] + table[:, 4] + table[:, 5]
    mean, inv = combine_groups(means, squares, rows * cols, channels)
    scale = inv * gain_ref[...].reshape(1, channels)
    shift = shift_ref[...].reshape(1, channels)

    def act(raw):
        u = (raw.astype(F32) - mean) * scale + shift
        return u / (1.0 + jnp.exp(-u))

    base = 8
    flat = lat_ref[...].reshape(rows * cols, channels)
    pad_ref[1 : rows + 1, base : base + cols] = act(flat).reshape(rows, cols, channels)
    for a, b in AROUND:
        inside, slot = slot_of(grid_rows, grid_cols, a, b)
        values = jnp.where(inside, act(near_ref[slot, :, :channels]), 0.0)
        line = 0 if a < 0 else rows + 1
        pixel = base - 1 if b < 0 else base + cols
        if b == 0:
            pad_ref[line, base : base + cols] = values
        elif a == 0:
            for i in range(rows):
                pad_ref[1 + i, pixel : pixel + 1] = values[i : i + 1]
        else:
            pad_ref[line, pixel : pixel + 1] = values[0:1]
    shifted = [pad_ref[:, base + b - 1 : base + b - 1 + cols].astype(BF16) for b in range(3)]
    depth = 3 * channels
    total = None
    for t in range(3):
        window = jnp.concatenate(
            [s[t : t + rows].reshape(rows * cols, channels) for s in shifted], axis=1
        )
        part = jnp.dot(window, w_ref[pl.ds(t * depth, depth), :], preferred_element_type=F32)
        total = part if total is None else total + part
    update = total.astype(BF16)
    conv_ref[...] = update.reshape(rows, cols, channels)
    stream = (flat.astype(F32) + update.astype(F32)).astype(BF16)
    stream_ref[...] = stream
    mean, square = local_moments(stream.astype(F32))
    out_stat_ref[...] = jnp.broadcast_to(
        jnp.concatenate([mean, square], axis=0)[None], out_stat_ref.shape
    )


def normalise(block, affine):
    return ((block.astype(F32) - affine[0:1]) * affine[1:2] + affine[2:3]).astype(BF16)


def project(blocks, affine, wk_ref, wvt_ref, key_ref, value_ref, start=0):
    raw = jnp.concatenate(blocks, axis=0) if len(blocks) > 1 else blocks[0]
    normed = normalise(raw, affine)
    place = slice(start, start + raw.shape[0])
    key_ref[place] = jnp.dot(normed, wk_ref[...], preferred_element_type=F32).astype(BF16)
    value_ref[:, place] = lax.dot_general(
        wvt_ref[...], normed, NT, preferred_element_type=F32
    ).astype(BF16)


def stacked(values):
    return jnp.concatenate([values, jnp.ones((16, values.shape[1]), BF16)], axis=0)


def attend(low, top, key_ref, value_ref, qbd, put):
    scores = jnp.dot(key_ref[:, low : low + 2 * HEAD], qbd, preferred_element_type=F32)
    weights = jnp.exp2(scores - top).astype(BF16)
    queries = scores.shape[1] // 2
    for h in range(2):
        put(h, jnp.dot(
            stacked(value_ref[low + HEAD * h : low + HEAD * h + HEAD]),
            weights[:, h * queries : (h + 1) * queries],
            preferred_element_type=F32,
        ))
    return jnp.max(scores.reshape(-1, 8, 2 * queries), axis=0)


def attend_again(low, top, key_ref, value_ref, qbd, put):
    scores = jnp.dot(key_ref[:, pl.ds(low, 2 * HEAD)], qbd, preferred_element_type=F32)
    new = jnp.maximum(top, jnp.max(scores, axis=0, keepdims=True))
    weights = jnp.exp2(scores - new).astype(BF16)
    rescale = jnp.exp2(top - new)
    queries = scores.shape[1] // 2
    for h in range(2):
        side = slice(h * queries, (h + 1) * queries)
        put(h, rescale[:, side], jnp.dot(
            stacked(value_ref[pl.ds(low + HEAD * h, HEAD)]), weights[:, side],
            preferred_element_type=F32,
        ))
    return new


def fetch(sources, held_ref, sems):
    copies = [
        pltpu.make_async_copy(source, held_ref.at[i], sems.at[i])
        for i, source in enumerate(sources)
    ]
    for copy in copies:
        copy.start()
    return copies


def first_kernel(
    own_any, x0_any, yp_any, peer_any, stat_ref, gain_ref, shift_ref, wqt_ref, wk_ref,
    wvt_ref, aff_ref, qbd_ref, acc_ref, max_ref, key_ref, value_ref, held_ref, sems,
):
    copies = fetch([own_any, peer_any, x0_any, yp_any], held_ref, sems)
    _, length, channels = held_ref.shape
    pairs = channels // (2 * HEAD)
    queries = 2 * length
    stats = stat_ref[...]
    mean, inv = combine_moments(stats[:, 0], stats[:, 1], length)
    affine = row_stack(
        [mean, inv * gain_ref[...].reshape(1, channels), shift_ref[...].reshape(1, channels)], 8
    )
    aff_ref[...] = affine
    for copy in copies:
        copy.wait()
    own = held_ref[0]
    normed = normalise(jnp.concatenate([own, held_ref[1]], axis=0), affine)
    factor = math.log2(math.e) / math.sqrt(HEAD)
    qt = (
        lax.dot_general(wqt_ref[...], normed, NT, preferred_element_type=F32) * factor
    ).astype(BF16)
    zero = jnp.zeros((HEAD, queries), BF16)
    blocks = [own] + [held_ref[i] for i in range(2, 4)]
    project(blocks, affine, wk_ref, wvt_ref, key_ref, value_ref)
    for j in range(pairs):
        low = 2 * HEAD * j
        qbd = jnp.concatenate(
            [
                jnp.concatenate([qt[low : low + HEAD], zero], axis=1),
                jnp.concatenate([zero, qt[low + HEAD : low + 2 * HEAD]], axis=1),
            ],
            axis=0,
        )
        qbd_ref[j] = qbd
        few = jnp.dot(key_ref[0:LANES, low : low + 2 * HEAD], qbd, preferred_element_type=F32)
        max_ref[j] = jnp.max(few, axis=0, keepdims=True)
    excess = None
    for j in range(pairs):

        def put(h, value):
            acc_ref[2 * j + h] = value

        high = attend(2 * HEAD * j, max_ref[j], key_ref, value_ref, qbd_ref[j], put)
        over = high - max_ref[j]
        excess = over if excess is None else jnp.maximum(excess, over)

    @pl.when(jnp.max(excess) > HEADROOM)
    def _():
        def one_pair(j, _):
            def put(h, rescale, value):
                acc_ref[2 * j + h] = value

            low = pl.multiple_of(2 * HEAD * j, 2 * HEAD)
            max_ref[j] = attend_again(low, max_ref[j], key_ref, value_ref, qbd_ref[j], put)
            return 0

        lax.fori_loop(0, pairs, one_pair, 0)


def more_kernel(head, tail, *refs):
    count = head + tail
    here, elsewhere = refs[:head], refs[head:count]
    aff_ref, qbd_ref, acc_in, max_in, wk_ref, wvt_ref, acc_ref, max_ref = refs[count : count + 8]
    key_ref, value_ref, held_ref, sems = refs[count + 8 :]
    copies = fetch(elsewhere, held_ref, sems)
    heads, _, queries = acc_in.shape
    pairs = heads // 2
    work = (aff_ref[...], wk_ref, wvt_ref, key_ref, value_ref)
    project([b[...] for b in here], *work)
    for copy in copies:
        copy.wait()
    project([held_ref[i] for i in range(tail)], *work, start=head * held_ref.shape[1])
    excess = None
    for j in range(pairs):

        def put(h, value):
            acc_ref[2 * j + h] = acc_in[2 * j + h] + value

        high = attend(2 * HEAD * j, max_in[j], key_ref, value_ref, qbd_ref[j], put)
        over = high - max_in[j]
        excess = over if excess is None else jnp.maximum(excess, over)
    max_ref[...] = max_in[...]

    @pl.when(jnp.max(excess) > HEADROOM)
    def _():
        def one_pair(j, _):
            def put(h, rescale, value):
                acc_ref[2 * j + h] = acc_in[2 * j + h] * rescale + value

            low = pl.multiple_of(2 * HEAD * j, 2 * HEAD)
            max_ref[j] = attend_again(low, max_in[j], key_ref, value_ref, qbd_ref[j], put)
            return 0

        lax.fori_loop(0, pairs, one_pair, 0)


def half_of(values, side):
    queries = values.shape[1] // 2
    half = queries // 2
    starts = [h * queries + side * half for h in range(2)]
    return jnp.concatenate([values[:, s : s + half] for s in starts], axis=1)


def attend_half(side, key_ref, value_ref, qbd_ref, acc_in, max_in, acc_ref, max_ref):
    heads, _, queries = acc_in.shape
    half = queries // 2
    lanes = slice(side * half, (side + 1) * half)
    excess = None
    for j in range(heads // 2):

        def put(h, value):
            acc_ref[2 * j + h] = acc_in[2 * j + h, :, lanes] + value

        top = half_of(max_in[j], side)
        high = attend(2 * HEAD * j, top, key_ref, value_ref, half_of(qbd_ref[j], side), put)
        over = high - top
        excess = over if excess is None else jnp.maximum(excess, over)
        max_ref[j] = top

    @pl.when(jnp.max(excess) > HEADROOM)
    def _():
        def one_pair(j, _):
            def put(h, rescale, value):
                acc_ref[2 * j + h] = acc_in[2 * j + h, :, lanes] * rescale + value

            low = pl.multiple_of(2 * HEAD * j, 2 * HEAD)
            max_ref[j] = attend_again(
                low, half_of(max_in[j], side), key_ref, value_ref, half_of(qbd_ref[j], side), put
            )
            return 0

        lax.fori_loop(0, heads // 2, one_pair, 0)


def give_kernel(count, *refs):
    blocks = refs[:count]
    aff_ref, qbd_ref, acc_in, max_in, wk_ref, wvt_ref = refs[count : count + 6]
    give_ref, key_ref, value_ref, acc_ref, max_ref = refs[count + 6 :]
    project([b[...] for b in blocks], aff_ref[...], wk_ref, wvt_ref, key_ref, value_ref)
    attend_half(1, key_ref, value_ref, qbd_ref, acc_in, max_in, acc_ref, max_ref)
    heads, _, half = acc_ref.shape
    logs = []
    for head in range(heads):
        j, h = head // 2, head % 2
        total = acc_ref[head, HEAD : HEAD + 1]
        give_ref[HEAD * head : HEAD * head + HEAD] = (acc_ref[head, 0:HEAD] / total).astype(BF16)
        logs.append(
            max_ref[j, :, h * half : (h + 1) * half] + jnp.log(total) * math.log2(math.e)
        )
    value = jnp.concatenate(logs + [jnp.zeros((16 - heads, half), F32)], axis=0)
    base = HEAD * heads
    for i in range(3):
        part = value.astype(BF16)
        give_ref[base + 16 * i : base + 16 * i + 16] = part
        value = value - part.astype(F32)


def keep_kernel(key_ref, value_ref, qbd_ref, acc_in, max_in, acc_ref, max_ref):
    attend_half(0, key_ref, value_ref, qbd_ref, acc_in, max_in, acc_ref, max_ref)


def join_kernel(acc_ref, max_ref, got_ref, wo_ref, out_ref):
    heads, _, half = acc_ref.shape
    base = HEAD * heads
    logs = sum(got_ref[base + 16 * i : base + 16 * i + 16].astype(F32) for i in range(3))
    parts = []
    for head in range(heads):
        j, h = head // 2, head % 2
        top = max_ref[j, :, h * half : (h + 1) * half]
        other = logs[head : head + 1]
        both = jnp.maximum(top, other)
        mine, theirs = jnp.exp2(top - both), jnp.exp2(other - both)
        total = acc_ref[head, HEAD : HEAD + 1] * mine + theirs
        inverse = 1.0 / total
        found = got_ref[HEAD * head : HEAD * head + HEAD].astype(F32)
        parts.append(
            (acc_ref[head, 0:HEAD] * (mine * inverse) + found * (theirs * inverse)).astype(BF16)
        )
    attended = jnp.concatenate(parts, axis=0)
    out_ref[...] = lax.dot_general(attended, wo_ref[...], TN, preferred_element_type=F32).astype(
        BF16
    )


def shift_by(value, axis, step):
    count = lax.axis_size(axis)
    return lax.ppermute(value, axis, [(i, (i + step) % count) for i in range(count)])


def shards(
    latent, norm1_gain, norm1_shift, conv_weight, norm2_gain, norm2_shift,
    w_query, w_key, w_value, w_out,
):
    rows, cols, channels = latent.shape
    local = rows * cols
    heads = channels // HEAD
    pairs = heads // 2
    devices = math.prod(lax.axis_size(a) for a in PARTS)
    sds = jax.ShapeDtypeStruct
    grid = (lax.axis_size("row"), lax.axis_size("x") * lax.axis_size("core"))
    vm = pl.BlockSpec(memory_space=pltpu.VMEM)

    tie = lax.optimization_barrier
    slots = pl.pallas_call(
        lambda *refs: edge_kernel(*grid, *refs),
        in_specs=[vm],
        out_specs=vm,
        out_shape=sds((devices, rows, channels + LANES), BF16),
        cost_estimate=cost(2),
        compiler_params=params(8 * 2**20),
    )(latent)
    near = lax.all_to_all(slots, PARTS, 0, 0)
    near, wqt, wvt = tie((near, w_query.T, w_value.T))
    conv_update, stream, moments2 = pl.pallas_call(
        lambda *refs: conv_kernel(*grid, *refs),
        in_specs=[vm] * 5,
        out_specs=[vm] * 3,
        out_shape=[
            sds((rows, cols, channels), BF16),
            sds((local, channels), BF16),
            sds((devices, 2, channels), F32),
        ],
        scratch_shapes=[pltpu.VMEM((rows + 2, cols + 16, channels), F32)],
        cost_estimate=cost(5),
        compiler_params=params(),
    )(latent, near, norm1_gain, norm1_shift, conv_weight.reshape(9 * channels, channels))

    swap = lambda v: shift_by(v, "core", 1)
    cross = lambda v: shift_by(v, "x", 1)
    up = lambda v: shift_by(v, "row", 1)
    down = lambda v: shift_by(v, "row", -1)
    own_peer = swap(stream)
    x0, ym, yp = cross(stream), up(stream), down(stream)
    gathered2 = lax.all_to_all(moments2, PARTS, 0, 0)
    span = lax.axis_size("row")
    far = [
        (2 * y + x, 2 * ((y + span // 2) % span) + 1 - x) for y in range(span) for x in range(2)
    ]
    x2 = lax.ppermute(stream, ("row", "x"), far)
    xm, y2, xp = cross(ym), up(ym), down(x0)

    state = [
        sds((heads, HEAD + 16, 2 * local), F32),
        sds((pairs, 1, 4 * local), F32),
    ]
    work = lambda keys, blocks: [
        pltpu.VMEM((keys * local, channels), BF16),
        pltpu.VMEM((channels, keys * local), BF16),
        pltpu.VMEM((blocks, local, channels), BF16),
        pltpu.SemaphoreType.DMA((blocks,)),
    ]
    anywhere = pl.BlockSpec(memory_space=pl.ANY)

    affine, qbd, acc, top_scores = pl.pallas_call(
        first_kernel,
        out_shape=[sds((8, channels), F32), sds((pairs, 2 * HEAD, 4 * local), BF16)] + state,
        in_specs=[anywhere] * 4 + [vm] * 6,
        scratch_shapes=work(3, 4),
        compiler_params=params(),
        cost_estimate=cost(9),
    )(stream, x0, yp, own_peer, gathered2, norm2_gain, norm2_shift, wqt, w_key, wvt)

    def more(here, elsewhere, acc, top_scores):
        head, tail = len(here), len(elsewhere)
        count = head + tail
        return pl.pallas_call(
            lambda *refs: more_kernel(head, tail, *refs),
            out_shape=state,
            in_specs=[vm] * head + [anywhere] * tail + [vm] * 6,
            scratch_shapes=work(count, tail),
            compiler_params=params(),
            cost_estimate=cost(2 * count),
        )(*here, *elsewhere, affine, qbd, acc, top_scores, w_key, wvt)

    acc, top_scores = more([ym], [x2], acc, top_scores)
    blocks = [xm, xp, y2]
    count = len(blocks)
    half_state = [sds((heads, HEAD + 16, local), F32), sds((pairs, 1, 2 * local), F32)]
    give, keys, values = pl.pallas_call(
        lambda *refs: give_kernel(count, *refs),
        out_shape=[
            sds((channels + 3 * 16, local), BF16),
            sds((count * local, channels), BF16),
            sds((channels, count * local), BF16),
        ],
        scratch_shapes=[pltpu.VMEM(s.shape, s.dtype) for s in half_state],
        compiler_params=params(),
        cost_estimate=cost(4),
    )(*blocks, affine, qbd, acc, top_scores, w_key, wvt)
    got = swap(give)
    acc, top_scores = pl.pallas_call(
        keep_kernel, out_shape=half_state, compiler_params=params(), cost_estimate=cost(3)
    )(keys, values, qbd, acc, top_scores)
    attn = pl.pallas_call(
        join_kernel, out_shape=sds((local, channels), BF16), compiler_params=params()
    )(acc, top_scores, got, w_out)
    return conv_update, attn.reshape(rows, cols, channels)


def solution(mesh):
    sizes = dict(mesh.shape)
    split = Mesh(
        mesh.devices.reshape(sizes["batch"], sizes["row"], sizes["col"] // 2, 2),
        ("batch", "row", "x", "core"),
    )
    tiles = P(("batch", "row"), ("x", "core"), None)
    return jax.shard_map(
        shards,
        mesh=split,
        in_specs=(tiles,) + (P(),) * 9,
        out_specs=(tiles, tiles),
        check_vma=False,
    )
```

```python
import math

import jax
import jax.numpy as jnp
from jax import lax
from jax.experimental import pallas as pl
from jax.experimental.pallas import tpu as pltpu
from jax.sharding import Mesh
from jax.sharding import PartitionSpec as P

GROUPS = 32
HEAD = 64
EPS = 1e-05
F32 = jnp.float32
BF16 = jnp.bfloat16
NT = (((1,), (1,)), ((), ()))
TN = (((0,), (0,)), ((), ()))
PARTS = ("row", "x", "core")
LANES = 128
VMEM_LIMIT = 28 * 2**20
HEADROOM = 64.0


def cost(us):
    return pl.CostEstimate(flops=int(us * 1e9), bytes_accessed=0, transcendentals=0)


def params(limit=VMEM_LIMIT):
    return pltpu.CompilerParams(vmem_limit_bytes=limit)


def member(rows_are_channels, channels):
    per_group = channels // GROUPS
    shape = (channels, LANES) if rows_are_channels else (LANES, channels)
    channel = lax.broadcasted_iota(jnp.int32, shape, 0 if rows_are_channels else 1)
    group = lax.broadcasted_iota(jnp.int32, shape, 1 if rows_are_channels else 0)
    inside = (channel >= group * per_group) & (channel < (group + 1) * per_group)
    return jnp.where(inside, 1.0, 0.0).astype(BF16)


def planes_of(value):
    parts = []
    for _ in range(3):
        part = value.astype(BF16).astype(F32)
        parts.append(part)
        value = value - part
    return parts


def row_stack(rows, count):
    pad = [jnp.zeros((count - len(rows), rows[0].shape[1]), F32)] if len(rows) < count else []
    return jnp.concatenate(rows + pad, axis=0)


def through(vectors, one_hot):
    rows = [part for vector in vectors for part in planes_of(vector)]
    out = jnp.dot(row_stack(rows, 16).astype(BF16), one_hot, preferred_element_type=F32)
    return [
        out[3 * i : 3 * i + 1] + out[3 * i + 1 : 3 * i + 2] + out[3 * i + 2 : 3 * i + 3]
        for i in range(len(vectors))
    ]


def local_moments(values):
    mean = jnp.sum(values, axis=0, keepdims=True) * (1.0 / values.shape[0])
    off = values - mean
    return mean, jnp.sum(off * off, axis=0, keepdims=True)


def combine_moments(means, squares, local_pixels):
    devices, channels = means.shape
    per_group = channels // GROUPS
    pixels = devices * local_pixels
    mean_c = jnp.sum(means, axis=0, keepdims=True) * (1.0 / devices)
    off = means - mean_c
    square_c = jnp.sum(squares, axis=0, keepdims=True) + local_pixels * jnp.sum(
        off * off, axis=0, keepdims=True
    )
    to_group, to_channel = member(True, channels), member(False, channels)
    (sum_g,) = through([mean_c], to_group)
    (mean,) = through([sum_g * (1.0 / per_group)], to_channel)
    gap = mean_c - mean
    (square_g,) = through([square_c + pixels * (gap * gap)], to_group)
    inv = 1.0 / jnp.sqrt(square_g * (1.0 / (pixels * per_group)) + EPS)
    (inv,) = through([inv], to_channel)
    return mean, inv


def group_moments(values):
    count, channels = values.shape
    mean_c, square_c = local_moments(values)
    to_group, to_channel = member(True, channels), member(False, channels)
    sum_g, square_g = through([mean_c, square_c], to_group)
    mean_g = sum_g * (GROUPS / channels)
    (wide,) = through([mean_g], to_channel)
    gap = mean_c - wide
    (spread,) = through([gap * gap], to_group)
    return mean_g, square_g + count * spread


def combine_groups(means, squares, local_pixels, channels):
    devices = means.shape[0]
    count = local_pixels * (channels // GROUPS)
    mean = jnp.sum(means, axis=0, keepdims=True) * (1.0 / devices)
    off = means - mean
    square = jnp.sum(squares, axis=0, keepdims=True) + count * jnp.sum(
        off * off, axis=0, keepdims=True
    )
    inv = 1.0 / jnp.sqrt(square * (1.0 / (devices * count)) + EPS)
    return through([mean, inv], member(False, channels))


def place():
    return lax.axis_index("row"), lax.axis_index("x") * lax.axis_size("core") + lax.axis_index("core")


AROUND = [(a, b) for a in (-1, 0, 1) for b in (-1, 0, 1) if (a, b) != (0, 0)]


def slot_of(grid_rows, grid_cols, a, b):
    row, col = place()
    inside = (row + a >= 0) & (row + a < grid_rows) & (col + b >= 0) & (col + b < grid_cols)
    return inside, jnp.where(inside, (row + a) * grid_cols + col + b, 0)


def edge_kernel(grid_rows, grid_cols, lat_ref, out_ref):
    rows, cols, channels = lat_ref.shape
    lat = lat_ref[...]
    mean, square = group_moments(lat.reshape(rows * cols, channels).astype(F32))
    table = row_stack(planes_of(mean) + planes_of(square), rows).astype(BF16)
    out_ref[:, :, channels:] = jnp.broadcast_to(table[None], (out_ref.shape[0], rows, LANES))
    for a, b in AROUND:
        inside, slot = slot_of(grid_rows, grid_cols, a, b)

        @pl.when(inside)
        def _(a=a, b=b, slot=slot):
            line = 0 if a < 0 else rows - 1
            pixel = 0 if b < 0 else cols - 1
            if b == 0:
                edge = lat[line]
            elif a == 0:
                edge = lat[:, pixel]
            else:
                edge = jnp.broadcast_to(lat[line, pixel : pixel + 1], (rows, channels))
            out_ref[pl.ds(slot, 1), :, :channels] = edge[None]


def conv_kernel(
    grid_rows, grid_cols, lat_ref, near_ref, gain_ref, shift_ref, w_ref,
    conv_ref, stream_ref, out_stat_ref, pad_ref,
):
    rows, cols, channels = lat_ref.shape
    table = near_ref[:, :, channels:].astype(F32)
    means = table[:, 0] + table[:, 1] + table[:, 2]
    squares = table[:, 3] + table[:, 4] + table[:, 5]
    mean, inv = combine_groups(means, squares, rows * cols, channels)
    scale = inv * gain_ref[...].reshape(1, channels)
    shift = shift_ref[...].reshape(1, channels)

    def act(raw):
        u = (raw.astype(F32) - mean) * scale + shift
        return u / (1.0 + jnp.exp(-u))

    base = 8
    flat = lat_ref[...].reshape(rows * cols, channels)
    pad_ref[1 : rows + 1, base : base + cols] = act(flat).reshape(rows, cols, channels)
    for a, b in AROUND:
        inside, slot = slot_of(grid_rows, grid_cols, a, b)
        values = jnp.where(inside, act(near_ref[slot, :, :channels]), 0.0)
        line = 0 if a < 0 else rows + 1
        pixel = base - 1 if b < 0 else base + cols
        if b == 0:
            pad_ref[line, base : base + cols] = values
        elif a == 0:
            for i in range(rows):
                pad_ref[1 + i, pixel : pixel + 1] = values[i : i + 1]
        else:
            pad_ref[line, pixel : pixel + 1] = values[0:1]
    shifted = [pad_ref[:, base + b - 1 : base + b - 1 + cols].astype(BF16) for b in range(3)]
    depth = 3 * channels
    total = None
    for t in range(3):
        window = jnp.concatenate(
            [s[t : t + rows].reshape(rows * cols, channels) for s in shifted], axis=1
        )
        part = jnp.dot(window, w_ref[pl.ds(t * depth, depth), :], preferred_element_type=F32)
        total = part if total is None else total + part
    update = total.astype(BF16)
    conv_ref[...] = update.reshape(rows, cols, channels)
    stream = (flat.astype(F32) + update.astype(F32)).astype(BF16)
    stream_ref[...] = stream
    mean, square = local_moments(stream.astype(F32))
    out_stat_ref[...] = jnp.broadcast_to(
        jnp.concatenate([mean, square], axis=0)[None], out_stat_ref.shape
    )


def normalise(block, affine):
    return ((block.astype(F32) - affine[0:1]) * affine[1:2] + affine[2:3]).astype(BF16)


def project(blocks, affine, wk_ref, wvt_ref, key_ref, value_ref, start=0):
    raw = jnp.concatenate(blocks, axis=0) if len(blocks) > 1 else blocks[0]
    normed = normalise(raw, affine)
    place = slice(start, start + raw.shape[0])
    key_ref[place] = jnp.dot(normed, wk_ref[...], preferred_element_type=F32).astype(BF16)
    value_ref[:, place] = lax.dot_general(
        wvt_ref[...], normed, NT, preferred_element_type=F32
    ).astype(BF16)


def stacked(values):
    return jnp.concatenate([values, jnp.ones((8, values.shape[1]), BF16)], axis=0)


def attend(low, top, key_ref, value_ref, qbd, put):
    scores = jnp.dot(key_ref[:, low : low + 2 * HEAD], qbd, preferred_element_type=F32)
    weights = jnp.exp2(scores - top).astype(BF16)
    queries = scores.shape[1] // 2
    for h in range(2):
        put(h, jnp.dot(
            stacked(value_ref[low + HEAD * h : low + HEAD * h + HEAD]),
            weights[:, h * queries : (h + 1) * queries],
            preferred_element_type=F32,
        ))
    return jnp.max(scores.reshape(-1, 8, 2 * queries), axis=0)


def attend_again(low, top, key_ref, value_ref, qbd, put):
    scores = jnp.dot(key_ref[:, pl.ds(low, 2 * HEAD)], qbd, preferred_element_type=F32)
    new = jnp.maximum(top, jnp.max(scores, axis=0, keepdims=True))
    weights = jnp.exp2(scores - new).astype(BF16)
    rescale = jnp.exp2(top - new)
    queries = scores.shape[1] // 2
    for h in range(2):
        side = slice(h * queries, (h + 1) * queries)
        put(h, rescale[:, side], jnp.dot(
            stacked(value_ref[pl.ds(low + HEAD * h, HEAD)]), weights[:, side],
            preferred_element_type=F32,
        ))
    return new


def fetch(sources, held_ref, sems):
    copies = [
        pltpu.make_async_copy(source, held_ref.at[i], sems.at[i])
        for i, source in enumerate(sources)
    ]
    for copy in copies:
        copy.start()
    return copies


def first_kernel(
    own_any, x0_any, yp_any, peer_any, stat_ref, gain_ref, shift_ref, wqt_ref, wk_ref,
    wvt_ref, aff_ref, qbd_ref, acc_ref, max_ref, key_ref, value_ref, held_ref, sems,
):
    copies = fetch([own_any, peer_any, x0_any, yp_any], held_ref, sems)
    _, length, channels = held_ref.shape
    pairs = channels // (2 * HEAD)
    queries = 2 * length
    stats = stat_ref[...]
    mean, inv = combine_moments(stats[:, 0], stats[:, 1], length)
    affine = row_stack(
        [mean, inv * gain_ref[...].reshape(1, channels), shift_ref[...].reshape(1, channels)], 8
    )
    aff_ref[...] = affine
    for copy in copies:
        copy.wait()
    own = held_ref[0]
    normed = normalise(jnp.concatenate([own, held_ref[1]], axis=0), affine)
    factor = math.log2(math.e) / math.sqrt(HEAD)
    qt = (
        lax.dot_general(wqt_ref[...], normed, NT, preferred_element_type=F32) * factor
    ).astype(BF16)
    zero = jnp.zeros((HEAD, queries), BF16)
    blocks = [own] + [held_ref[i] for i in range(2, 4)]
    project(blocks, affine, wk_ref, wvt_ref, key_ref, value_ref)
    for j in range(pairs):
        low = 2 * HEAD * j
        qbd = jnp.concatenate(
            [
                jnp.concatenate([qt[low : low + HEAD], zero], axis=1),
                jnp.concatenate([zero, qt[low + HEAD : low + 2 * HEAD]], axis=1),
            ],
            axis=0,
        )
        qbd_ref[j] = qbd
        few = jnp.dot(key_ref[0:LANES, low : low + 2 * HEAD], qbd, preferred_element_type=F32)
        max_ref[j] = jnp.max(few, axis=0, keepdims=True)
    excess = None
    for j in range(pairs):

        def put(h, value):
            acc_ref[2 * j + h] = value

        high = attend(2 * HEAD * j, max_ref[j], key_ref, value_ref, qbd_ref[j], put)
        over = high - max_ref[j]
        excess = over if excess is None else jnp.maximum(excess, over)

    @pl.when(jnp.max(excess) > HEADROOM)
    def _():
        def one_pair(j, _):
            def put(h, rescale, value):
                acc_ref[2 * j + h] = value

            low = pl.multiple_of(2 * HEAD * j, 2 * HEAD)
            max_ref[j] = attend_again(low, max_ref[j], key_ref, value_ref, qbd_ref[j], put)
            return 0

        lax.fori_loop(0, pairs, one_pair, 0)


def more_kernel(head, tail, *refs):
    count = head + tail
    here, elsewhere = refs[:head], refs[head:count]
    aff_ref, qbd_ref, acc_in, max_in, wk_ref, wvt_ref, acc_ref, max_ref = refs[count : count + 8]
    key_ref, value_ref, held_ref, sems = refs[count + 8 :]
    copies = fetch(elsewhere, held_ref, sems)
    heads, _, queries = acc_in.shape
    pairs = heads // 2
    work = (aff_ref[...], wk_ref, wvt_ref, key_ref, value_ref)
    project([b[...] for b in here], *work)
    for copy in copies:
        copy.wait()
    project([held_ref[i] for i in range(tail)], *work, start=head * held_ref.shape[1])
    excess = None
    for j in range(pairs):

        def put(h, value):
            acc_ref[2 * j + h] = acc_in[2 * j + h] + value

        high = attend(2 * HEAD * j, max_in[j], key_ref, value_ref, qbd_ref[j], put)
        over = high - max_in[j]
        excess = over if excess is None else jnp.maximum(excess, over)
    max_ref[...] = max_in[...]

    @pl.when(jnp.max(excess) > HEADROOM)
    def _():
        def one_pair(j, _):
            def put(h, rescale, value):
                acc_ref[2 * j + h] = acc_in[2 * j + h] * rescale + value

            low = pl.multiple_of(2 * HEAD * j, 2 * HEAD)
            max_ref[j] = attend_again(low, max_in[j], key_ref, value_ref, qbd_ref[j], put)
            return 0

        lax.fori_loop(0, pairs, one_pair, 0)


def half_of(values, side):
    queries = values.shape[1] // 2
    half = queries // 2
    starts = [h * queries + side * half for h in range(2)]
    return jnp.concatenate([values[:, s : s + half] for s in starts], axis=1)


def attend_half(side, key_ref, value_ref, qbd_ref, acc_in, max_in, acc_ref, max_ref):
    heads, _, queries = acc_in.shape
    half = queries // 2
    lanes = slice(side * half, (side + 1) * half)
    excess = None
    for j in range(heads // 2):

        def put(h, value):
            acc_ref[2 * j + h] = acc_in[2 * j + h, :, lanes] + value

        top = half_of(max_in[j], side)
        high = attend(2 * HEAD * j, top, key_ref, value_ref, half_of(qbd_ref[j], side), put)
        over = high - top
        excess = over if excess is None else jnp.maximum(excess, over)
        max_ref[j] = top

    @pl.when(jnp.max(excess) > HEADROOM)
    def _():
        def one_pair(j, _):
            def put(h, rescale, value):
                acc_ref[2 * j + h] = acc_in[2 * j + h, :, lanes] * rescale + value

            low = pl.multiple_of(2 * HEAD * j, 2 * HEAD)
            max_ref[j] = attend_again(
                low, half_of(max_in[j], side), key_ref, value_ref, half_of(qbd_ref[j], side), put
            )
            return 0

        lax.fori_loop(0, heads // 2, one_pair, 0)


def give_kernel(count, *refs):
    blocks = refs[:count]
    aff_ref, qbd_ref, acc_in, max_in, wk_ref, wvt_ref = refs[count : count + 6]
    give_ref, key_ref, value_ref, acc_ref, max_ref = refs[count + 6 :]
    project([b[...] for b in blocks], aff_ref[...], wk_ref, wvt_ref, key_ref, value_ref)
    attend_half(1, key_ref, value_ref, qbd_ref, acc_in, max_in, acc_ref, max_ref)
    heads, _, half = acc_ref.shape
    logs = []
    for head in range(heads):
        j, h = head // 2, head % 2
        total = acc_ref[head, HEAD : HEAD + 1]
        give_ref[HEAD * head : HEAD * head + HEAD] = (acc_ref[head, 0:HEAD] / total).astype(BF16)
        logs.append(
            max_ref[j, :, h * half : (h + 1) * half] + jnp.log(total) * math.log2(math.e)
        )
    value = jnp.concatenate(logs + [jnp.zeros((16 - heads, half), F32)], axis=0)
    base = HEAD * heads
    for i in range(3):
        part = value.astype(BF16)
        give_ref[base + 16 * i : base + 16 * i + 16] = part
        value = value - part.astype(F32)


def keep_kernel(key_ref, value_ref, qbd_ref, acc_in, max_in, acc_ref, max_ref):
    attend_half(0, key_ref, value_ref, qbd_ref, acc_in, max_in, acc_ref, max_ref)


def join_kernel(acc_ref, max_ref, got_ref, wo_ref, out_ref):
    heads, _, half = acc_ref.shape
    base = HEAD * heads
    logs = sum(got_ref[base + 16 * i : base + 16 * i + 16].astype(F32) for i in range(3))
    parts = []
    for head in range(heads):
        j, h = head // 2, head % 2
        top = max_ref[j, :, h * half : (h + 1) * half]
        other = logs[head : head + 1]
        both = jnp.maximum(top, other)
        mine, theirs = jnp.exp2(top - both), jnp.exp2(other - both)
        total = acc_ref[head, HEAD : HEAD + 1] * mine + theirs
        inverse = 1.0 / total
        found = got_ref[HEAD * head : HEAD * head + HEAD].astype(F32)
        parts.append(
            (acc_ref[head, 0:HEAD] * (mine * inverse) + found * (theirs * inverse)).astype(BF16)
        )
    attended = jnp.concatenate(parts, axis=0)
    out_ref[...] = lax.dot_general(attended, wo_ref[...], TN, preferred_element_type=F32).astype(
        BF16
    )


def shift_by(value, axis, step):
    count = lax.axis_size(axis)
    return lax.ppermute(value, axis, [(i, (i + step) % count) for i in range(count)])


def shards(
    latent, norm1_gain, norm1_shift, conv_weight, norm2_gain, norm2_shift,
    w_query, w_key, w_value, w_out,
):
    rows, cols, channels = latent.shape
    local = rows * cols
    heads = channels // HEAD
    pairs = heads // 2
    devices = math.prod(lax.axis_size(a) for a in PARTS)
    sds = jax.ShapeDtypeStruct
    grid = (lax.axis_size("row"), lax.axis_size("x") * lax.axis_size("core"))
    vm = pl.BlockSpec(memory_space=pltpu.VMEM)

    tie = lax.optimization_barrier
    slots = pl.pallas_call(
        lambda *refs: edge_kernel(*grid, *refs),
        in_specs=[vm],
        out_specs=vm,
        out_shape=sds((devices, rows, channels + LANES), BF16),
        cost_estimate=cost(2),
        compiler_params=params(8 * 2**20),
    )(latent)
    near = lax.all_to_all(slots, PARTS, 0, 0)
    near, wqt, wvt = tie((near, w_query.T, w_value.T))
    conv_update, stream, moments2 = pl.pallas_call(
        lambda *refs: conv_kernel(*grid, *refs),
        in_specs=[vm] * 5,
        out_specs=[vm] * 3,
        out_shape=[
            sds((rows, cols, channels), BF16),
            sds((local, channels), BF16),
            sds((devices, 2, channels), F32),
        ],
        scratch_shapes=[pltpu.VMEM((rows + 2, cols + 16, channels), F32)],
        cost_estimate=cost(5),
        compiler_params=params(),
    )(latent, near, norm1_gain, norm1_shift, conv_weight.reshape(9 * channels, channels))

    swap = lambda v: shift_by(v, "core", 1)
    cross = lambda v: shift_by(v, "x", 1)
    up = lambda v: shift_by(v, "row", 1)
    down = lambda v: shift_by(v, "row", -1)
    own_peer = swap(stream)
    x0, ym, yp = cross(stream), up(stream), down(stream)
    gathered2 = lax.all_to_all(moments2, PARTS, 0, 0)
    span = lax.axis_size("row")
    far = [
        (2 * y + x, 2 * ((y + span // 2) % span) + 1 - x) for y in range(span) for x in range(2)
    ]
    x2 = lax.ppermute(stream, ("row", "x"), far)
    xm, y2, xp = cross(ym), up(ym), down(x0)

    state = [
        sds((heads, HEAD + 8, 2 * local), F32),
        sds((pairs, 1, 4 * local), F32),
    ]
    work = lambda keys, blocks: [
        pltpu.VMEM((keys * local, channels), BF16),
        pltpu.VMEM((channels, keys * local), BF16),
        pltpu.VMEM((blocks, local, channels), BF16),
        pltpu.SemaphoreType.DMA((blocks,)),
    ]
    anywhere = pl.BlockSpec(memory_space=pl.ANY)

    affine, qbd, acc, top_scores = pl.pallas_call(
        first_kernel,
        out_shape=[sds((8, channels), F32), sds((pairs, 2 * HEAD, 4 * local), BF16)] + state,
        in_specs=[anywhere] * 4 + [vm] * 6,
        scratch_shapes=work(3, 4),
        compiler_params=params(),
        cost_estimate=cost(9),
    )(stream, x0, yp, own_peer, gathered2, norm2_gain, norm2_shift, wqt, w_key, wvt)

    def more(here, elsewhere, acc, top_scores):
        head, tail = len(here), len(elsewhere)
        count = head + tail
        return pl.pallas_call(
            lambda *refs: more_kernel(head, tail, *refs),
            out_shape=state,
            in_specs=[vm] * head + [anywhere] * tail + [vm] * 6,
            scratch_shapes=work(count, tail),
            compiler_params=params(),
            cost_estimate=cost(2 * count),
        )(*here, *elsewhere, affine, qbd, acc, top_scores, w_key, wvt)

    acc, top_scores = more([ym], [x2], acc, top_scores)
    blocks = [xm, xp, y2]
    count = len(blocks)
    half_state = [sds((heads, HEAD + 8, local), F32), sds((pairs, 1, 2 * local), F32)]
    give, keys, values = pl.pallas_call(
        lambda *refs: give_kernel(count, *refs),
        out_shape=[
            sds((channels + 3 * 16, local), BF16),
            sds((count * local, channels), BF16),
            sds((channels, count * local), BF16),
        ],
        scratch_shapes=[pltpu.VMEM(s.shape, s.dtype) for s in half_state],
        compiler_params=params(),
        cost_estimate=cost(4),
    )(*blocks, affine, qbd, acc, top_scores, w_key, wvt)
    got = swap(give)
    acc, top_scores = pl.pallas_call(
        keep_kernel, out_shape=half_state, compiler_params=params(), cost_estimate=cost(3)
    )(keys, values, qbd, acc, top_scores)
    attn = pl.pallas_call(
        join_kernel, out_shape=sds((local, channels), BF16), compiler_params=params()
    )(acc, top_scores, got, w_out)
    return conv_update, attn.reshape(rows, cols, channels)


def solution(mesh):
    sizes = dict(mesh.shape)
    split = Mesh(
        mesh.devices.reshape(sizes["batch"], sizes["row"], sizes["col"] // 2, 2),
        ("batch", "row", "x", "core"),
    )
    tiles = P(("batch", "row"), ("x", "core"), None)
    return jax.shard_map(
        shards,
        mesh=split,
        in_specs=(tiles,) + (P(),) * 9,
        out_specs=(tiles, tiles),
        check_vma=False,
    )
```
